32 devices in a mesh: tm: 4 (over y, x), sta: 8 (over z, core).
Axes of the slice: x: 2, y: 2, z: 4, core: 2. Of those that a mesh axis runs over, the one named last changes fastest.
Arguments:
- spectra: bfloat16 [4, 8, 2, 3, 2, 2048], P('tm', 'sta'), may hold values from -6 to 6
- pair_blocks: int32 [8, 8, 2], P('sta'), may hold values from 0 to 7, as said below
- block_count: int32 [8], P('sta'), may hold values from 1 to 8, as said below
Outputs:
- correlations: bfloat16 [8, 8, 1, 1, 3, 3, 4096], P('sta', 'tm')
The draws below stay inside these ranges and needn't reach their ends.
Inputs may be any that keep to these rules, and one draw needn't show every extreme that they name: `pair_blocks`: among the first block_count[o] slots of all owners o, every unordered pair of two different station groups stands exactly once, in either order; later slots hold arbitrary group numbers. `block_count`: the counts sum to 28, and one owner uses all 8 slots.
All inputs are finite; a program needn't handle non-finite values.
Results may differ from the reference program's by a relative error of at most 0.014.
Values may be sent and summed in bfloat16 or wider, within the bound.
No kernel may reach another device: no remote copies, remote signals or barrier semaphores. Data moves between devices by JAX's collectives and lax.ppermute only.
A program may use at most 64 MiB of HBM per device.

```python
import jax
import jax.numpy as jnp
import numpy as np
from jax import lax

F = 2048
LAGS = 4096
SMOOTH = 64
STA_DEV = 1
SEGS = 2
HOURS = 4
GROUPS = 8
STATIONS = 8
SLOTS = 8


def owner_plan(key):
    pair_total = GROUPS * (GROUPS - 1) // 2
    key_rank, key_weight, key_order, key_filler, key_flip = jax.random.split(jax.random.fold_in(key, 11), 5)
    owner_rank = jax.random.permutation(key_rank, GROUPS)
    ranks = jnp.arange(GROUPS, dtype=jnp.int32)
    weights = jax.random.randint(key_weight, (GROUPS,), 2, 4, dtype=jnp.int32)
    weights = jnp.where(ranks == 0, 0, weights)
    remaining = pair_total - SLOTS
    shares = remaining * weights // jnp.sum(weights)
    leftover = remaining - jnp.sum(shares)
    shares = shares + ((ranks >= 1) & (ranks <= leftover)).astype(jnp.int32)
    by_rank = jnp.where(ranks == 0, SLOTS, shares).astype(jnp.int32)
    counts = jnp.zeros((GROUPS,), jnp.int32).at[owner_rank].set(by_rank)
    offsets = jnp.cumsum(counts) - counts
    upper_pairs = np.triu_indices(GROUPS, 1)
    first_all = jnp.asarray(upper_pairs[0], dtype=jnp.int32)
    second_all = jnp.asarray(upper_pairs[1], dtype=jnp.int32)
    order = jax.random.permutation(key_order, pair_total)
    flipped = jax.random.randint(key_flip, (pair_total,), 0, 2, dtype=jnp.int32) == 1
    first_pick = jnp.where(flipped, second_all[order], first_all[order])
    second_pick = jnp.where(flipped, first_all[order], second_all[order])
    slot_positions = jnp.arange(SLOTS, dtype=jnp.int32)[None, :]
    slot_index = offsets[:, None] + slot_positions
    live = slot_positions < counts[:, None]
    safe_index = jnp.minimum(slot_index, pair_total - 1)
    pairs = jnp.stack([first_pick[safe_index], second_pick[safe_index]], axis=-1)
    filler = jax.random.randint(key_filler, (GROUPS, SLOTS, 2), 0, GROUPS, dtype=jnp.int32)
    blocks = jnp.where(live[..., None], pairs, filler).astype(jnp.int32)
    return (blocks, counts)


def draw_pair_blocks(key, part):
    return owner_plan(key)[0]


def draw_block_count(key, part):
    return owner_plan(key)[1]


def steps_of(stream_key, dims, shards, smallest, high):
    def one(dim, blocks):
        heights = jax.random.uniform(jax.random.fold_in(jax.random.fold_in(stream_key, 6), dim), (blocks,), jnp.float32, smallest / len(shards), high / len(shards))
        return jnp.repeat(jnp.exp(heights), dims[dim] // blocks).reshape((-1,) + (1,) * (len(dims) - dim - 1))

    gain = one(*shards[0])
    for cut in shards[1:]:
        gain = gain * one(*cut)
    return gain


def centred(own_key, extent, deviation, most, cuts=(), held_as=jnp.bfloat16):
    array = jax.random.normal(own_key, extent, jnp.float32) * deviation
    if len(cuts) > 0:
        array = steps_of(own_key, extent, cuts, -0.22, 0.18) * array
    return jnp.clip(array, min=-most, max=most).astype(held_as)


def setup_inputs(seed: int = 0) -> dict:
    streams_of = jax.random.split(jax.random.key(seed), 4)
    return {
        "spectra": centred(streams_of[0], (HOURS, STATIONS, SEGS, 3, 2, F), 1.0, 6.0, ((0, 4), (1, 8))),
        "pair_blocks": draw_pair_blocks(jax.random.fold_in(streams_of[3], 71), 0),
        "block_count": draw_block_count(jax.random.fold_in(streams_of[3], 71), 0),
    }


epsilon = 1e-05

def whiten(spectra):
    values = spectra.astype(jnp.float32)
    amplitude = jnp.sqrt(values[..., 0, :] ** 2 + values[..., 1, :] ** 2)
    width = amplitude.shape[-1]
    padding = [(0, 0)] * (amplitude.ndim - 1) + [(SMOOTH + 1, SMOOTH)]
    running = jnp.cumsum(jnp.pad(amplitude, padding), axis=-1)
    window_sum = running[..., 2 * SMOOTH + 1:] - running[..., :width]
    positions = jnp.arange(width, dtype=jnp.int32)
    lower = jnp.maximum(positions - SMOOTH, 0)
    upper = jnp.minimum(positions + SMOOTH, width - 1)
    bin_count = (upper - lower + 1).astype(jnp.float32)
    smoothed = window_sum / bin_count
    white = values / (smoothed + epsilon)[..., None, :]
    return white.astype(jnp.bfloat16)

def cross_hours(every, firsts, seconds):
    grouped = every.reshape(every.shape[0], GROUPS, STA_DEV, SEGS, 3, 2, F)
    left = grouped[:, firsts].astype(jnp.float32)
    right = grouped[:, seconds].astype(jnp.float32)
    form = 'hnasxf,hnbsyf->hnabxyf'
    high = lax.Precision.HIGHEST
    real_part = jnp.einsum(form, left[..., 0, :], right[..., 0, :], precision=high) + jnp.einsum(form, left[..., 1, :], right[..., 1, :], precision=high)
    imag_part = jnp.einsum(form, left[..., 0, :], right[..., 1, :], precision=high) - jnp.einsum(form, left[..., 1, :], right[..., 0, :], precision=high)
    return jnp.stack([real_part, imag_part], axis=-2)

def lag_values(daily):
    values = daily.astype(jnp.float32)
    spectrum = lax.complex(values[..., 0, :], values[..., 1, :])
    inverse = jnp.fft.ifft(spectrum, n=LAGS, axis=-1)
    scaled = jnp.real(inverse) * (LAGS * F ** (-0.5))
    return jnp.roll(scaled, F, axis=-1).astype(jnp.bfloat16)

def reference(spectra, pair_blocks, block_count):
    white = whiten(spectra)

    def one_owner(owner_args):
        blocks, live_count = owner_args
        partial_value = cross_hours(white, blocks[:, 0], blocks[:, 1]).astype(jnp.bfloat16)
        daily = lax.optimization_barrier(jnp.sum(partial_value.astype(jnp.float32), axis=0))
        live = (jnp.arange(SLOTS, dtype=jnp.int32) < live_count).astype(jnp.float32)
        daily = (daily * live[:, None, None, None, None, None, None]).astype(jnp.bfloat16)
        return lag_values(daily)
    return lax.map(one_owner, (pair_blocks, block_count))
```

```python
import functools
import math

import jax
import jax.numpy as jnp
import numpy as np
from jax import lax
from jax.experimental import pallas as pl
from jax.experimental.pallas import tpu as pltpu
from jax.sharding import PartitionSpec as P

SMOOTH = 64
LANES = 128
PARTS = 3
SLAB = 8

epsilon = 1e-05
MESH_AXES = ("tm", "sta")
VMEM = pl.BlockSpec(memory_space=pltpu.VMEM)


def kernel_call(kernel, out_shape, operands, scratch):
    return pl.pallas_call(
        kernel,
        out_shape=out_shape,
        in_specs=[VMEM] * operands,
        out_specs=VMEM,
        scratch_shapes=scratch,
        compiler_params=pltpu.CompilerParams(vmem_limit_bytes=40 * 1024 * 1024),
    )


def whiten_kernel(segments, owners, x_ref, o_ref, rows):
    shards, _, width = x_ref.shape
    run = width // segments
    reach = SMOOTH // shards
    lane = lax.broadcasted_iota(jnp.int32, (SLAB, width), 1) % run

    def moved(value, step):
        inside = (lane + step >= 0) & (lane + step < run)
        return jnp.where(inside, pltpu.roll(value, (-step) % width, 1), 0.0)

    values, sizes = [], []
    for d in range(shards):
        value = x_ref[d].astype(jnp.float32)
        square = value * value
        values.append(value)
        sizes.append(jnp.sqrt(square + pltpu.roll(square, 4, 0)))
    upto, beyond = [sizes[0]], [sizes[-1]]
    for d in range(1, shards):
        upto.append(upto[-1] + sizes[d])
        beyond.append(beyond[-1] + sizes[shards - 1 - d])
    beyond = beyond[::-1]
    middle = upto[-1]
    for step in range(1, reach):
        middle = middle + (moved(upto[-1], step) + moved(upto[-1], -step))
    bins = run * shards
    for d in range(shards):
        window = middle + (moved(beyond[d], -reach) + moved(upto[d], reach))
        place = lane * shards + d
        count = jnp.minimum(place + SMOOTH, bins - 1) - jnp.maximum(place - SMOOTH, 0) + 1
        smoothed = window / count.astype(jnp.float32)
        white = values[d] / (smoothed + epsilon)
        for v in range(width // LANES):
            for c in range(2):
                first = (v * 2 + c) * PARTS
                rows[d, first : first + PARTS] = white[c * 4 : c * 4 + PARTS, v * LANES : (v + 1) * LANES]
    packed = rows[...].astype(jnp.bfloat16)
    for device, d in enumerate(owners):
        o_ref[device] = packed[d]


def cross_kernel(segments, share, pick_ref, w_ref, o_ref, rows):
    hours, depth, _ = w_ref.shape
    slots = pick_ref.shape[1]
    group = slots // share
    chunk = o_ref.shape[1]
    kinds = 2 * PARTS
    halves = chunk // (share * PARTS * PARTS * 2)
    blocks = segments * halves * kinds
    column = lax.broadcasted_iota(jnp.int32, (slots, depth), 1)
    sides = []
    for side in range(2):
        offset = column - pick_ref[side]
        sides.append([(offset == r).astype(jnp.bfloat16) for r in range(blocks)])
    chosen = jnp.concatenate(sides[0] + sides[1], axis=0)
    picked = [
        jnp.dot(chosen, w_ref[h], preferred_element_type=jnp.float32) for h in range(hours)
    ]

    def part(side, h, g, j, c, x):
        first = (side * blocks + ((g * halves + j) * 2 + c) * PARTS + x) * slots
        return picked[h][first : first + slots]

    for j in range(halves):
        real = [None] * (PARTS * PARTS)
        imag = [None] * (PARTS * PARTS)
        for h in range(hours):
            for g in range(segments):
                left = [[part(0, h, g, j, c, x) for x in range(PARTS)] for c in range(2)]
                right = [[part(1, h, g, j, c, x) for x in range(PARTS)] for c in range(2)]
                for x in range(PARTS):
                    for y in range(PARTS):
                        re = left[0][x] * right[0][y] + left[1][x] * right[1][y]
                        im = left[0][x] * right[1][y] - left[1][x] * right[0][y]
                        n = x * PARTS + y
                        real[n] = re if real[n] is None else real[n] + re
                        imag[n] = im if imag[n] is None else imag[n] + im
        for n in range(PARTS * PARTS):
            for c, total in enumerate((real[n], imag[n])):
                for u in range(share):
                    row = ((u * PARTS * PARTS + n) * 2 + c) * halves + j
                    rows[pl.ds(row, group, stride=chunk), :] = total[u * group : (u + 1) * group]
    o_ref[...] = rows[...].reshape(o_ref.shape).astype(jnp.bfloat16)


def lag_kernel(live_ref, d_ref, first_ref, cos_ref, sin_ref, second_ref, o_ref, rows):
    lines, period = cos_ref.shape
    pieces = d_ref.shape[0] // lines
    share = o_ref.shape[0]
    rows[...] = d_ref[...].astype(jnp.float32)
    daily = jnp.concatenate(
        [rows[pl.ds(k, lines, stride=pieces), :].astype(jnp.bfloat16) for k in range(pieces)], axis=1
    )
    middle = jnp.dot(daily, first_ref[...], preferred_element_type=jnp.float32)
    re, im = middle[:, :period], middle[:, period:]
    turned = jnp.concatenate(
        [
            (re * cos_ref[...] - im * sin_ref[...]).astype(jnp.bfloat16),
            (re * sin_ref[...] + im * cos_ref[...]).astype(jnp.bfloat16),
        ],
        axis=0,
    )
    joined = jnp.dot(second_ref[...], turned, preferred_element_type=jnp.float32)
    turns = joined.shape[0] // (share * PARTS * SLAB)
    for a in range(turns):
        for u in range(share):
            for x in range(PARTS):
                first = ((a * share + u) * PARTS + x) * SLAB
                value = jnp.where(live_ref[u] > 0, joined[first : first + PARTS], 0.0)
                o_ref[u, x, :, a * period : (a + 1) * period] = value.astype(jnp.bfloat16)


def lag_tables(bins, shards, share):
    lags = 2 * bins
    period = lags // shards
    per_slot = PARTS * PARTS
    k = np.arange(bins // shards)[:, None]
    b = np.arange(period)[None, :]
    angle = (k * b % period) * (2.0 * math.pi / period)
    cos, sin = np.cos(angle), np.sin(angle)
    first = np.block([[cos, sin], [-sin, cos]])
    d = np.arange(shards)[:, None]
    angle = np.repeat(d * b * (2.0 * math.pi / lags), share * per_slot, axis=0)
    scale = bins**-0.5
    a = np.arange(shards)[:, None] - bins // period
    turn = (a * d.T % shards) * (2.0 * math.pi / shards)
    line = np.eye(share * per_slot).reshape(share, PARTS, PARTS, -1)
    line = np.pad(line, ((0, 0), (0, 0), (0, SLAB - PARTS), (0, 0))).reshape(-1, share * per_slot)
    second = [
        np.einsum("ad,mr->amdr", table, line).reshape(shards * line.shape[0], -1)
        for table in (np.cos(turn), -np.sin(turn))
    ]
    return (
        jnp.asarray(first, jnp.bfloat16),
        jnp.asarray(np.cos(angle) * scale, jnp.float32),
        jnp.asarray(np.sin(angle) * scale, jnp.float32),
        jnp.asarray(np.concatenate(second, axis=1), jnp.bfloat16),
    )


def body(spectra, pair_blocks, block_count):
    _, _, segments, parts, _, bins = spectra.shape
    slots = pair_blocks.shape[1]
    hours, stations = lax.axis_size("tm"), lax.axis_size("sta")
    near = 2
    shards = hours * near
    share = slots // hours
    run = bins // shards
    halves = run // LANES
    chunk_in = segments * halves * 2 * parts
    chunk_out = share * parts * parts * 2 * halves

    def shard(t, s):
        return t * near + s % near

    swap = [(s, s ^ 1) for s in range(stations)]
    other = lax.ppermute(pair_blocks, "sta", swap)
    is_second = lax.axis_index("sta") % near == 1
    both = jnp.where(is_second, jnp.concatenate([other, pair_blocks]), jnp.concatenate([pair_blocks, other]))
    lists = both.reshape(near, hours, share, 2).transpose(3, 2, 1, 0).reshape(2, share * shards, 1)
    depth = stations * chunk_in
    pick = jnp.broadcast_to(lists * chunk_in, (2, share * shards, depth))

    strided = spectra[0, 0].reshape(segments, parts, 2, run, shards).transpose(4, 2, 1, 0, 3)
    strided = jnp.pad(strided, ((0, 0), (0, 0), (0, 1), (0, 0), (0, 0)))
    strided = strided.reshape(shards, SLAB, segments * run)

    owners = [shard(t, s) for t in range(hours) for s in range(stations)]
    white = kernel_call(
        functools.partial(whiten_kernel, segments, owners),
        jax.ShapeDtypeStruct((hours * stations, chunk_in, LANES), jnp.bfloat16),
        1,
        [pltpu.VMEM((shards, chunk_in, LANES), jnp.float32)],
    )(strided)
    every = lax.all_to_all(white, MESH_AXES, 0, 0, tiled=True)

    daily = kernel_call(
        functools.partial(cross_kernel, segments, share),
        jax.ShapeDtypeStruct((shards, chunk_out, LANES), jnp.bfloat16),
        2,
        [pltpu.VMEM((shards * chunk_out, LANES), jnp.float32)],
    )(pick, every.reshape(hours, depth, LANES))

    groups = [
        [t * stations + s + e for t in range(hours) for e in range(near)] for s in range(0, stations, near)
    ]
    mine = lax.all_to_all(daily, MESH_AXES, 0, 0, tiled=True, axis_index_groups=groups)

    first_slot = lax.axis_index("tm") * share
    live = (first_slot + jnp.arange(share, dtype=jnp.int32) < block_count[0]).astype(jnp.int32)
    result = pl.pallas_call(
        lag_kernel,
        out_shape=jax.ShapeDtypeStruct((share, parts, parts, 2 * bins), jnp.bfloat16),
        in_specs=[pl.BlockSpec(memory_space=pltpu.SMEM)] + [VMEM] * 5,
        out_specs=VMEM,
        scratch_shapes=[pltpu.VMEM((shards * chunk_out, LANES), jnp.float32)],
        compiler_params=pltpu.CompilerParams(vmem_limit_bytes=40 * 1024 * 1024),
    )(live, mine.reshape(shards * chunk_out, LANES), *lag_tables(bins, shards, share))
    return result.reshape(1, share, 1, 1, parts, parts, 2 * bins)


def solution(mesh):
    placed = (P("tm", "sta", None, None, None, None), P("sta", None, None), P("sta"))
    return jax.shard_map(
        body,
        mesh=mesh,
        in_specs=placed,
        out_specs=P("sta", "tm", None, None, None, None, None),
        check_vma=False,
    )
```

```python
import functools
import math

import jax
import jax.numpy as jnp
import numpy as np
from jax import lax
from jax.experimental import pallas as pl
from jax.experimental.pallas import tpu as pltpu
from jax.sharding import PartitionSpec as P

SMOOTH = 64
LANES = 128
PARTS = 3
SLAB = 8

epsilon = 1e-05
MESH_AXES = ("tm", "sta")
VMEM = pl.BlockSpec(memory_space=pltpu.VMEM)
HBM = pl.BlockSpec(memory_space=pltpu.HBM)


def in_hbm(array):
    return pltpu.with_memory_space_constraint(array, pltpu.HBM)


def kernel_call(kernel, out_shape, in_specs, scratch):
    return pl.pallas_call(
        kernel,
        out_shape=out_shape,
        in_specs=in_specs,
        out_specs=jax.tree.map(lambda _: VMEM, out_shape),
        scratch_shapes=scratch,
        compiler_params=pltpu.CompilerParams(vmem_limit_bytes=40 * 1024 * 1024),
    )


def whiten_kernel(
    owners, shards, segments, spectra_ref, pairs_ref, count_ref, o_ref, mine_ref, live_ref, x_ref, rows, sems
):
    bins = x_ref.shape[2]
    tiles = bins // LANES
    copies = [
        pltpu.make_async_copy(source, target, sems.at[n])
        for n, (source, target) in enumerate(((spectra_ref, x_ref), (pairs_ref, mine_ref)))
    ]
    for copy in copies:
        copy.start()
    lane = lax.broadcasted_iota(jnp.int32, (SLAB, LANES), 1)
    even = lax.broadcasted_iota(jnp.int32, (SLAB, LANES), 0) % 2 == 0
    turn = [lane % shards == k for k in range(shards)]
    blank = jnp.zeros((SLAB, LANES), jnp.float32)
    apart = lax.broadcasted_iota(jnp.int32, (3 * LANES, LANES), 0) - LANES
    apart = apart - lax.broadcasted_iota(jnp.int32, (3 * LANES, LANES), 1)
    band = (jnp.abs(apart) <= SMOOTH).astype(jnp.bfloat16)
    copies[0].wait()
    values, blocks = [], []
    for g in range(segments):
        lines = [x_ref[g * PARTS + x].astype(jnp.float32) for x in range(PARTS)]
        lines = jnp.concatenate(lines + [jnp.zeros((SLAB - 2 * PARTS, bins), jnp.float32)], axis=0)
        value = [lines[:, v * LANES : (v + 1) * LANES] for v in range(tiles)]
        size = [blank]
        for v in range(tiles):
            square = value[v] * value[v]
            twin = jnp.where(even, pltpu.roll(square, SLAB - 1, 0), pltpu.roll(square, 1, 0))
            size.append(jnp.sqrt(square + twin))
        size.append(blank)
        values.append(value)
        blocks += [jnp.concatenate(size[v : v + 3], axis=1) for v in range(tiles)]
    stacked = jnp.concatenate(blocks, axis=0)
    high = stacked.astype(jnp.bfloat16)
    low = (stacked - high.astype(jnp.float32)).astype(jnp.bfloat16)
    window = jnp.dot(high, band, preferred_element_type=jnp.float32) + jnp.dot(
        low, band, preferred_element_type=jnp.float32
    )
    halves = tiles // shards
    for g in range(segments):
        for j in range(halves):
            moved = []
            for i in range(shards):
                v = j * shards + i
                place = lane + v * LANES
                count = jnp.minimum(place + SMOOTH, bins - 1) - jnp.maximum(place - SMOOTH, 0) + 1
                first = (g * tiles + v) * SLAB
                smoothed = window[first : first + SLAB] / count.astype(jnp.float32)
                white = values[g][v] / (smoothed + epsilon)
                moved.append(pltpu.roll(white, i, 1) if i else white)
            first = (g * halves + j) * 2 * PARTS
            for d in range(shards):
                mixed = moved[0]
                for i in range(1, shards):
                    mixed = jnp.where(turn[(d + i) % shards], moved[i], mixed)
                if d:
                    mixed = pltpu.roll(mixed, LANES - d, 1)
                rows[d, first : first + 2 * PARTS] = mixed[: 2 * PARTS]
    packed = rows[...].astype(jnp.bfloat16)
    for device, d in enumerate(owners):
        o_ref[device] = packed[d]
    copies[1].wait()
    live_ref[...] = jnp.full(live_ref.shape, count_ref[0])


def station_columns(pair_refs, hours, share):
    near = len(pair_refs)
    rows = share * hours * near
    lane = lax.broadcasted_iota(jnp.int32, (rows, hours * share), 1)
    row = lax.broadcasted_iota(jnp.int32, (rows, hours * share), 0)
    owner = row % near
    slot = row // near % hours * share + row // (near * hours)
    second = lax.axis_index("sta") % near == 1
    columns = []
    for side in range(2):
        mine, other = [jnp.broadcast_to(ref[side : side + 1], lane.shape) for ref in pair_refs]
        lists = [jnp.where(second, other, mine), jnp.where(second, mine, other)]
        value = jnp.where(owner == 1, lists[1], lists[0])
        columns.append(jnp.sum(jnp.where(lane == slot, value, 0), axis=1, keepdims=True))
    return columns


def cross_kernel(segments, share, mine_ref, other_ref, w_ref, table_ref, o_ref, held_ref, rows, sem):
    hours, depth, _ = w_ref.shape
    table_copy = pltpu.make_async_copy(table_ref, held_ref, sem)
    table_copy.start()
    group, chunk, _ = o_ref.shape
    slots = group * share
    kinds = 2 * PARTS
    halves = chunk // (share * PARTS * PARTS * 2)
    blocks = segments * halves * kinds
    column = lax.broadcasted_iota(jnp.int32, (slots, depth), 1)
    sides = []
    for station in station_columns((mine_ref, other_ref), hours, share):
        offset = column - station * blocks
        sides.append([(offset == r).astype(jnp.bfloat16) for r in range(blocks)])
    chosen = jnp.concatenate(sides[0] + sides[1], axis=0)
    picked = [
        jnp.dot(chosen, w_ref[h], preferred_element_type=jnp.float32) for h in range(hours)
    ]

    def part(side, h, g, j, c, x):
        first = (side * blocks + ((g * halves + j) * PARTS + x) * 2 + c) * slots
        return picked[h][first : first + slots]

    for j in range(halves):
        real = [None] * (PARTS * PARTS)
        imag = [None] * (PARTS * PARTS)
        for h in range(hours):
            for g in range(segments):
                left = [[part(0, h, g, j, c, x) for x in range(PARTS)] for c in range(2)]
                right = [[part(1, h, g, j, c, x) for x in range(PARTS)] for c in range(2)]
                for x in range(PARTS):
                    for y in range(PARTS):
                        re = left[0][x] * right[0][y] + left[1][x] * right[1][y]
                        im = left[0][x] * right[1][y] - left[1][x] * right[0][y]
                        n = x * PARTS + y
                        real[n] = re if real[n] is None else real[n] + re
                        imag[n] = im if imag[n] is None else imag[n] + im
        for n in range(PARTS * PARTS):
            for c, total in enumerate((real[n], imag[n])):
                for u in range(share):
                    row = ((u * PARTS * PARTS + n) * 2 + c) * halves + j
                    rows[pl.ds(row, group, stride=chunk), :] = total[u * group : (u + 1) * group]
    o_ref[...] = rows[...].reshape(o_ref.shape).astype(jnp.bfloat16)
    table_copy.wait()


def lag_kernel(live_ref, d_ref, table_ref, o_ref, rows):
    share, lags = o_ref.shape[2:]
    shards = lax.axis_size("tm") * 2
    period = lags // shards
    pieces = period // LANES
    lines = d_ref.shape[0] // (pieces * shards)
    total = lines * shards
    rows[...] = d_ref[...].astype(jnp.float32)
    daily = []
    for k in range(pieces):
        column = [rows[pl.ds(r * pieces + k, shards, stride=lines * pieces), :] for r in range(lines)]
        daily.append(jnp.concatenate(column, axis=0).astype(jnp.bfloat16))
    daily = jnp.concatenate(daily, axis=1)
    middle = jnp.dot(daily, table_ref[:period, : 2 * period], preferred_element_type=jnp.float32)
    middle = middle.reshape(lines, shards, 2 * period)
    re, im = middle[:, :, :period], middle[:, :, period:]
    turn = table_ref[period + total : period + total + 2 * shards, : 2 * period].astype(jnp.float32)
    turn = turn[:shards] + turn[shards:]
    cos, sin = turn[None, :, :period], turn[None, :, period:]
    turned = jnp.concatenate(
        [
            (re * cos - im * sin).reshape(total, period).astype(jnp.bfloat16),
            (re * sin + im * cos).reshape(total, period).astype(jnp.bfloat16),
        ],
        axis=0,
    )
    second = table_ref[period : period + total, : 2 * total]
    joined = jnp.dot(second, turned, preferred_element_type=jnp.float32)
    live = live_ref[:1, :1] - lax.axis_index("tm") * share
    slot = lax.broadcasted_iota(jnp.int32, joined.shape, 0) % share
    joined = jnp.where(slot < live, joined, 0.0)
    for a in range(shards):
        for n in range(PARTS * PARTS):
            first = (a * PARTS * PARTS + n) * share
            value = joined[first : first + share].astype(jnp.bfloat16)
            o_ref[n // PARTS, n % PARTS, :, a * period : (a + 1) * period] = value


def lag_table(bins, shards, share):
    lags = 2 * bins
    period = lags // shards
    lines = share * PARTS * PARTS
    lane = np.arange(LANES)
    inner = lane % shards * (LANES // shards) + lane // shards
    k = (np.arange(0, bins // shards, LANES)[:, None] + inner).reshape(-1, 1)
    b = np.arange(period)[None, :]
    angle = (k * b % period) * (2.0 * math.pi / period)
    cos, sin = np.cos(angle), np.sin(angle)
    first = np.block([[cos, sin], [-sin, cos]])
    d = np.arange(shards)[:, None]
    a = np.arange(shards)[:, None] - bins // period
    turn = (a * d.T % shards) * (2.0 * math.pi / shards)
    same = np.eye(lines).reshape(share, PARTS * PARTS, lines).transpose(1, 0, 2)
    second = [np.einsum("ad,nur->anurd", table, same) for table in (np.cos(turn), -np.sin(turn))]
    second = np.concatenate([table.reshape(lines * shards, -1) for table in second], axis=1)
    angle = d * b * (2.0 * math.pi / lags)
    fine = np.concatenate([np.cos(angle), np.sin(angle)], axis=1) * bins**-0.5
    high = fine.astype(jnp.bfloat16).astype(np.float64)
    fine = np.concatenate([high, fine - high])
    width = max(first.shape[1], second.shape[1], fine.shape[1])
    table = [np.pad(t, ((0, 0), (0, width - t.shape[1]))) for t in (first, second, fine)]
    return jnp.asarray(np.concatenate(table), jnp.bfloat16)


def body(spectra, pair_blocks, block_count):
    _, _, segments, parts, _, bins = spectra.shape
    slots = pair_blocks.shape[1]
    hours, stations = lax.axis_size("tm"), lax.axis_size("sta")
    near = 2
    shards = hours * near
    share = slots // hours
    run = bins // shards
    halves = run // LANES
    chunk_in = segments * halves * 2 * parts
    chunk_out = share * parts * parts * 2 * halves

    def shard(t, s):
        return t * near + s % near

    swap = [(s, s ^ 1) for s in range(stations)]
    pairs = pair_blocks[0].T
    other = lax.ppermute(pairs, "sta", swap)
    depth = stations * chunk_in

    owners = [shard(t, s) for t in range(hours) for s in range(stations)]
    white, mine, live = kernel_call(
        functools.partial(whiten_kernel, owners, shards, segments),
        (
            pltpu.VMEM((hours * stations, chunk_in, LANES), jnp.bfloat16),
            pltpu.VMEM((2, slots), jnp.int32),
            pltpu.VMEM((SLAB, LANES), jnp.int32),
        ),
        [HBM, HBM, pl.BlockSpec(memory_space=pltpu.SMEM)],
        [
            pltpu.VMEM((segments * parts, 2, bins), jnp.bfloat16),
            pltpu.VMEM((shards, chunk_in, LANES), jnp.float32),
            pltpu.SemaphoreType.DMA((2,)),
        ],
    )(in_hbm(spectra.reshape(segments * parts, 2, bins)), in_hbm(pairs), block_count)
    white, other = lax.optimization_barrier((white, other))
    every = lax.all_to_all(white, MESH_AXES, 0, 0, tiled=True)

    table = lag_table(bins, shards, share)
    daily, table = kernel_call(
        functools.partial(cross_kernel, segments, share),
        (
            pltpu.VMEM((shards, chunk_out, LANES), jnp.bfloat16),
            pltpu.VMEM(table.shape, table.dtype),
        ),
        [VMEM, VMEM, VMEM, HBM],
        [pltpu.VMEM((shards * chunk_out, LANES), jnp.float32), pltpu.SemaphoreType.DMA],
    )(mine, other, every.reshape(hours, depth, LANES), in_hbm(table))

    groups = [
        [t * stations + s + e for t in range(hours) for e in range(near)] for s in range(0, stations, near)
    ]
    whole = lax.all_to_all(daily, MESH_AXES, 0, 0, tiled=True, axis_index_groups=groups)

    result = kernel_call(
        lag_kernel,
        jax.ShapeDtypeStruct((parts, parts, share, 2 * bins), jnp.bfloat16),
        [VMEM] * 3,
        [pltpu.VMEM((shards * chunk_out, LANES), jnp.float32)],
    )(live, whole.reshape(shards * chunk_out, LANES), table)
    return result.transpose(2, 0, 1, 3).reshape(1, share, 1, 1, parts, parts, 2 * bins)


def solution(mesh):
    placed = (P("tm", "sta", None, None, None, None), P("sta", None, None), P("sta"))
    return jax.shard_map(
        body,
        mesh=mesh,
        in_specs=placed,
        out_specs=P("sta", "tm", None, None, None, None, None),
        check_vma=False,
    )
```

```python
import functools
import math

import jax
import jax.numpy as jnp
import numpy as np
from jax import lax
from jax.experimental import pallas as pl
from jax.experimental.pallas import tpu as pltpu
from jax.sharding import PartitionSpec as P

SMOOTH = 64
LANES = 128
PARTS = 3
SLAB = 8

epsilon = 1e-05
MESH_AXES = ("tm", "sta")
VMEM = pl.BlockSpec(memory_space=pltpu.VMEM)
HBM = pl.BlockSpec(memory_space=pltpu.HBM)


def in_hbm(array):
    return pltpu.with_memory_space_constraint(array, pltpu.HBM)


def kernel_call(kernel, out_shape, in_specs, scratch, out_spec=VMEM):
    return pl.pallas_call(
        kernel,
        out_shape=out_shape,
        in_specs=in_specs,
        out_specs=jax.tree.map(lambda _: out_spec, out_shape),
        scratch_shapes=scratch,
        compiler_params=pltpu.CompilerParams(vmem_limit_bytes=40 * 1024 * 1024),
    )


def whiten_kernel(
    owners, shards, segments, spectra_ref, pairs_ref, count_ref, *refs
):
    first_ref, second_ref, o_ref, mine_ref, live_ref, first_held, second_held, x_ref, rows, sems = refs
    bins = x_ref.shape[2]
    tiles = bins // LANES
    moves = [(spectra_ref.at[pl.ds(g * PARTS, PARTS)], x_ref.at[pl.ds(g * PARTS, PARTS)]) for g in range(segments)]
    moves += [(pairs_ref, mine_ref), (first_ref, first_held), (second_ref, second_held)]
    copies = [pltpu.make_async_copy(*move, sems.at[n]) for n, move in enumerate(moves)]
    for copy in copies:
        copy.start()
    lane = lax.broadcasted_iota(jnp.int32, (SLAB, LANES), 1)
    even = lax.broadcasted_iota(jnp.int32, (SLAB, LANES), 0) % 2 == 0
    turn = [lane % shards == k for k in range(shards)]
    blank = jnp.zeros((SLAB, LANES), jnp.float32)
    apart = lax.broadcasted_iota(jnp.int32, (3 * LANES, LANES), 0) - LANES
    apart = apart - lax.broadcasted_iota(jnp.int32, (3 * LANES, LANES), 1)
    band = (jnp.abs(apart) <= SMOOTH).astype(jnp.bfloat16)
    values, blocks = [], []
    for g in range(segments):
        copies[g].wait()
        lines = [x_ref[g * PARTS + x].astype(jnp.float32) for x in range(PARTS)]
        lines = jnp.concatenate(lines + [jnp.zeros((SLAB - 2 * PARTS, bins), jnp.float32)], axis=0)
        value = [lines[:, v * LANES : (v + 1) * LANES] for v in range(tiles)]
        size = [blank]
        for v in range(tiles):
            square = value[v] * value[v]
            twin = jnp.where(even, pltpu.roll(square, SLAB - 1, 0), pltpu.roll(square, 1, 0))
            size.append(jnp.sqrt(square + twin))
        size.append(blank)
        values.append(value)
        blocks += [jnp.concatenate(size[v : v + 3], axis=1) for v in range(tiles)]
    stacked = jnp.concatenate(blocks, axis=0)
    high = stacked.astype(jnp.bfloat16)
    low = (stacked - high.astype(jnp.float32)).astype(jnp.bfloat16)
    window = jnp.dot(high, band, preferred_element_type=jnp.float32) + jnp.dot(
        low, band, preferred_element_type=jnp.float32
    )
    halves = tiles // shards
    for g in range(segments):
        for j in range(halves):
            moved = []
            for i in range(shards):
                v = j * shards + i
                place = lane + v * LANES
                count = jnp.minimum(place + SMOOTH, bins - 1) - jnp.maximum(place - SMOOTH, 0) + 1
                first = (g * tiles + v) * SLAB
                smoothed = window[first : first + SLAB] / count.astype(jnp.float32)
                white = values[g][v] / (smoothed + epsilon)
                moved.append(pltpu.roll(white, i, 1) if i else white)
            first = (g * halves + j) * 2 * PARTS
            for d in range(shards):
                mixed = moved[0]
                for i in range(1, shards):
                    mixed = jnp.where(turn[(d + i) % shards], moved[i], mixed)
                if d:
                    mixed = pltpu.roll(mixed, LANES - d, 1)
                rows[d, first : first + 2 * PARTS] = mixed[: 2 * PARTS]
    packed = rows[...].astype(jnp.bfloat16)
    for device, d in enumerate(owners):
        o_ref[device] = packed[d]
    for copy in copies[segments:]:
        copy.wait()
    live_ref[...] = jnp.full(live_ref.shape, count_ref[0])


def station_columns(pair_refs, hours, share):
    near = len(pair_refs)
    rows = share * hours * near
    lane = lax.broadcasted_iota(jnp.int32, (rows, hours * share), 1)
    row = lax.broadcasted_iota(jnp.int32, (rows, hours * share), 0)
    owner = row % near
    slot = row // near % hours * share + row // (near * hours)
    second = lax.axis_index("sta") % near == 1
    columns = []
    for side in range(2):
        mine, other = [jnp.broadcast_to(ref[side : side + 1], lane.shape) for ref in pair_refs]
        lists = [jnp.where(second, other, mine), jnp.where(second, mine, other)]
        value = jnp.where(owner == 1, lists[1], lists[0])
        columns.append(jnp.sum(jnp.where(lane == slot, value, 0), axis=1, keepdims=True))
    return columns


def cross_kernel(segments, share, mine_ref, other_ref, w_ref, o_ref, rows):
    hours, depth, _ = w_ref.shape
    group, chunk, _ = o_ref.shape
    slots = group * share
    kinds = 2 * PARTS
    halves = chunk // (share * PARTS * PARTS * 2)
    blocks = segments * halves * kinds
    column = lax.broadcasted_iota(jnp.int32, (slots, depth), 1)
    sides = []
    for station in station_columns((mine_ref, other_ref), hours, share):
        offset = column - station * blocks
        sides.append([(offset == r).astype(jnp.bfloat16) for r in range(blocks)])
    chosen = jnp.concatenate(sides[0] + sides[1], axis=0)
    picked = []
    for h in range(0, hours, 2):
        two = jnp.concatenate([w_ref[e] for e in range(h, min(h + 2, hours))], axis=1)
        two = jnp.dot(chosen, two, preferred_element_type=jnp.float32)
        picked += [two[:, e : e + LANES] for e in range(0, two.shape[1], LANES)]

    def part(side, h, g, j, c, x):
        first = (side * blocks + ((g * halves + j) * PARTS + x) * 2 + c) * slots
        return picked[h][first : first + slots]

    for j in range(halves):
        real = [None] * (PARTS * PARTS)
        imag = [None] * (PARTS * PARTS)
        for h in range(hours):
            for g in range(segments):
                left = [[part(0, h, g, j, c, x) for x in range(PARTS)] for c in range(2)]
                right = [[part(1, h, g, j, c, x) for x in range(PARTS)] for c in range(2)]
                for x in range(PARTS):
                    for y in range(PARTS):
                        re = left[0][x] * right[0][y] + left[1][x] * right[1][y]
                        im = left[0][x] * right[1][y] - left[1][x] * right[0][y]
                        n = x * PARTS + y
                        real[n] = re if real[n] is None else real[n] + re
                        imag[n] = im if imag[n] is None else imag[n] + im
        for n in range(PARTS * PARTS):
            for c, total in enumerate((real[n], imag[n])):
                for u in range(share):
                    row = ((u * PARTS * PARTS + n) * 2 + c) * halves + j
                    rows[pl.ds(row, group, stride=chunk), :] = total[u * group : (u + 1) * group]
    o_ref[...] = rows[...].reshape(o_ref.shape).astype(jnp.bfloat16)


def lag_kernel(live_ref, d_ref, first_ref, second_ref, o_ref, rows, lags_ref, sems):
    share, lags = o_ref.shape[2:]
    shards = lax.axis_size("tm") * 2
    period = lags // shards
    pieces = period // LANES
    lines = d_ref.shape[0] // (pieces * shards)
    total = lines * shards
    rows[...] = d_ref[...].astype(jnp.float32)
    daily = []
    for k in range(pieces):
        column = [rows[pl.ds(r * pieces + k, shards, stride=lines * pieces), :] for r in range(lines)]
        daily.append(jnp.concatenate(column, axis=0).astype(jnp.bfloat16))
    half = pieces // 2
    daily = jnp.concatenate([jnp.concatenate(daily[c * half : (c + 1) * half], axis=1) for c in range(2)], axis=0)
    run = period // 2
    middle = jnp.dot(daily, first_ref[:run], preferred_element_type=jnp.float32)
    re = (middle[:total, :period] - middle[total:, period:]).reshape(lines, shards, period)
    im = (middle[:total, period:] + middle[total:, :period]).reshape(lines, shards, period)
    turn = first_ref[run : run + 2 * shards].astype(jnp.float32)
    turn = turn[:shards] + turn[shards:]
    cos, sin = turn[None, :, :period], turn[None, :, period:]
    turned = jnp.concatenate(
        [
            (re * cos - im * sin).reshape(total, period).astype(jnp.bfloat16),
            (re * sin + im * cos).reshape(total, period).astype(jnp.bfloat16),
        ],
        axis=0,
    )
    live = live_ref[:1, :1] - lax.axis_index("tm") * share
    cuts = sems.shape[0]
    depth = total // cuts
    slot = lax.broadcasted_iota(jnp.int32, (depth, period), 0) % share
    copies = []
    for cut in range(cuts):
        joined = jnp.dot(second_ref[cut * depth : (cut + 1) * depth], turned, preferred_element_type=jnp.float32)
        joined = jnp.where(slot < live, joined, 0.0)
        base = cut * (lags // cuts)
        for a in range(shards // cuts):
            for n in range(PARTS * PARTS):
                first = (a * PARTS * PARTS + n) * share
                value = joined[first : first + share].astype(jnp.bfloat16)
                lags_ref[n // PARTS, n % PARTS, :, base + a * period : base + (a + 1) * period] = value
        window = (slice(None),) * 3 + (pl.ds(base, lags // cuts),)
        copies.append(pltpu.make_async_copy(lags_ref.at[window], o_ref.at[window], sems.at[cut]))
        copies[-1].start()
    for copy in copies:
        copy.wait()


def lag_tables(bins, shards, share):
    lags = 2 * bins
    period = lags // shards
    lines = share * PARTS * PARTS
    lane = np.arange(LANES)
    inner = lane % shards * (LANES // shards) + lane // shards
    k = (np.arange(0, bins // shards, LANES)[:, None] + inner).reshape(-1, 1)
    b = np.arange(period)[None, :]
    d = np.arange(shards)[:, None]

    def turns(angle):
        return np.concatenate([np.cos(angle), np.sin(angle)], axis=1)

    fine = turns(d * b * (2.0 * math.pi / lags)) * bins**-0.5
    high = fine.astype(jnp.bfloat16).astype(np.float64)
    first = np.concatenate([turns((k * b % period) * (2.0 * math.pi / period)), high, fine - high])
    a = np.arange(shards)[:, None] - bins // period
    turn = (a * d.T % shards) * (2.0 * math.pi / shards)
    same = np.eye(lines).reshape(share, PARTS * PARTS, lines).transpose(1, 0, 2)
    second = [np.einsum("ad,nur->anurd", table, same) for table in (np.cos(turn), -np.sin(turn))]
    second = np.concatenate([table.reshape(lines * shards, -1) for table in second], axis=1)
    return jnp.asarray(first, jnp.bfloat16), jnp.asarray(second, jnp.bfloat16)


def body(spectra, pair_blocks, block_count):
    _, _, segments, parts, _, bins = spectra.shape
    slots = pair_blocks.shape[1]
    hours, stations = lax.axis_size("tm"), lax.axis_size("sta")
    near = 2
    shards = hours * near
    share = slots // hours
    run = bins // shards
    halves = run // LANES
    chunk_in = segments * halves * 2 * parts
    chunk_out = share * parts * parts * 2 * halves

    def shard(t, s):
        return t * near + s % near

    swap = [(s, s ^ 1) for s in range(stations)]
    pairs = pair_blocks[0].T
    other = lax.ppermute(pair_blocks, "sta", swap)[0].T
    depth = stations * chunk_in

    owners = [shard(t, s) for t in range(hours) for s in range(stations)]
    first, second = lag_tables(bins, shards, share)
    white, mine, live, first, second = kernel_call(
        functools.partial(whiten_kernel, owners, shards, segments),
        (
            pltpu.VMEM((hours * stations, chunk_in, LANES), jnp.bfloat16),
            pltpu.VMEM((2, slots), jnp.int32),
            pltpu.VMEM((SLAB, LANES), jnp.int32),
            pltpu.VMEM(first.shape, first.dtype),
            pltpu.VMEM(second.shape, second.dtype),
        ),
        [HBM, HBM, pl.BlockSpec(memory_space=pltpu.SMEM), HBM, HBM],
        [
            pltpu.VMEM((segments * parts, 2, bins), jnp.bfloat16),
            pltpu.VMEM((shards, chunk_in, LANES), jnp.float32),
            pltpu.SemaphoreType.DMA((segments + 3,)),
        ],
    )(
        in_hbm(spectra.reshape(segments * parts, 2, bins)),
        in_hbm(pairs),
        block_count,
        in_hbm(first),
        in_hbm(second),
    )
    white, other = lax.optimization_barrier((white, other))
    every = lax.all_to_all(white, MESH_AXES, 0, 0, tiled=True)

    daily = kernel_call(
        functools.partial(cross_kernel, segments, share),
        pltpu.VMEM((shards, chunk_out, LANES), jnp.bfloat16),
        [VMEM] * 3,
        [pltpu.VMEM((shards * chunk_out, LANES), jnp.float32)],
    )(mine, other, every.reshape(hours, depth, LANES))

    groups = [
        [t * stations + s + e for t in range(hours) for e in range(near)] for s in range(0, stations, near)
    ]
    whole = lax.all_to_all(daily, MESH_AXES, 0, 0, tiled=True, axis_index_groups=groups)

    result = kernel_call(
        lag_kernel,
        jax.ShapeDtypeStruct((parts, parts, share, 2 * bins), jnp.bfloat16),
        [VMEM] * 4,
        [
            pltpu.VMEM((shards * chunk_out, LANES), jnp.float32),
            pltpu.VMEM((parts, parts, share, 2 * bins), jnp.bfloat16),
            pltpu.SemaphoreType.DMA((2,)),
        ],
        pl.BlockSpec(memory_space=pl.ANY),
    )(live, whole.reshape(shards * chunk_out, LANES), first, second)
    return result.transpose(2, 0, 1, 3).reshape(1, share, 1, 1, parts, parts, 2 * bins)


def solution(mesh):
    placed = (P("tm", "sta", None, None, None, None), P("sta", None, None), P("sta"))
    return jax.shard_map(
        body,
        mesh=mesh,
        in_specs=placed,
        out_specs=P("sta", "tm", None, None, None, None, None),
        check_vma=False,
    )
```

```python
import functools
import math

import jax
import jax.numpy as jnp
import numpy as np
from jax import lax
from jax.experimental import pallas as pl
from jax.experimental.pallas import tpu as pltpu
from jax.sharding import PartitionSpec as P

SMOOTH = 64
LANES = 128
PARTS = 3
SLAB = 8

epsilon = 1e-05
MESH_AXES = ("tm", "sta")
VMEM = pl.BlockSpec(memory_space=pltpu.VMEM)
HBM = pl.BlockSpec(memory_space=pltpu.HBM)


def in_hbm(array):
    return pltpu.with_memory_space_constraint(array, pltpu.HBM)


def kernel_call(kernel, out_shape, in_specs, scratch, out_spec=VMEM):
    return pl.pallas_call(
        kernel,
        out_shape=out_shape,
        in_specs=in_specs,
        out_specs=jax.tree.map(lambda _: out_spec, out_shape),
        scratch_shapes=scratch,
        compiler_params=pltpu.CompilerParams(vmem_limit_bytes=40 * 1024 * 1024),
    )


def whiten_kernel(
    owners, shards, segments, spectra_ref, pairs_ref, count_ref, *refs
):
    first_ref, second_ref, o_ref, mine_ref, live_ref, first_held, second_held, x_ref, rows, sems = refs
    bins = x_ref.shape[2]
    tiles = bins // LANES
    moves = [(spectra_ref.at[pl.ds(g * PARTS, PARTS)], x_ref.at[pl.ds(g * PARTS, PARTS)]) for g in range(segments)]
    moves += [(pairs_ref, mine_ref), (first_ref, first_held), (second_ref, second_held)]
    copies = [pltpu.make_async_copy(*move, sems.at[n]) for n, move in enumerate(moves)]
    for copy in copies:
        copy.start()
    lane = lax.broadcasted_iota(jnp.int32, (SLAB, LANES), 1)
    even = lax.broadcasted_iota(jnp.int32, (SLAB, LANES), 0) % 2 == 0
    turn = [lane % shards == k for k in range(shards)]
    blank = jnp.zeros((SLAB, LANES), jnp.float32)
    apart = lax.broadcasted_iota(jnp.int32, (3 * LANES, LANES), 0) - LANES
    apart = apart - lax.broadcasted_iota(jnp.int32, (3 * LANES, LANES), 1)
    band = (jnp.abs(apart) <= SMOOTH).astype(jnp.bfloat16)
    values, blocks = [], []
    for g in range(segments):
        copies[g].wait()
        lines = [x_ref[g * PARTS + x].astype(jnp.float32) for x in range(PARTS)]
        lines = jnp.concatenate(lines + [jnp.zeros((SLAB - 2 * PARTS, bins), jnp.float32)], axis=0)
        value = [lines[:, v * LANES : (v + 1) * LANES] for v in range(tiles)]
        size = [blank]
        for v in range(tiles):
            square = value[v] * value[v]
            twin = jnp.where(even, pltpu.roll(square, SLAB - 1, 0), pltpu.roll(square, 1, 0))
            size.append(jnp.sqrt(square + twin))
        size.append(blank)
        values.append(value)
        blocks += [jnp.concatenate(size[v : v + 3], axis=1) for v in range(tiles)]
    stacked = jnp.concatenate(blocks, axis=0)
    high = stacked.astype(jnp.bfloat16)
    low = (stacked - high.astype(jnp.float32)).astype(jnp.bfloat16)
    window = jnp.dot(high, band, preferred_element_type=jnp.float32) + jnp.dot(
        low, band, preferred_element_type=jnp.float32
    )
    halves = tiles // shards
    for g in range(segments):
        for j in range(halves):
            moved = []
            for i in range(shards):
                v = j * shards + i
                place = lane + v * LANES
                count = jnp.minimum(place + SMOOTH, bins - 1) - jnp.maximum(place - SMOOTH, 0) + 1
                first = (g * tiles + v) * SLAB
                smoothed = window[first : first + SLAB] / count.astype(jnp.float32)
                white = values[g][v] / (smoothed + epsilon)
                moved.append(pltpu.roll(white, i, 1) if i else white)
            first = (g * halves + j) * 2 * PARTS
            for d in range(shards):
                mixed = moved[0]
                for i in range(1, shards):
                    mixed = jnp.where(turn[(d + i) % shards], moved[i], mixed)
                if d:
                    mixed = pltpu.roll(mixed, LANES - d, 1)
                rows[d, first : first + 2 * PARTS] = mixed[: 2 * PARTS]
    packed = rows[...].astype(jnp.bfloat16)
    for device, d in enumerate(owners):
        o_ref[device] = packed[d]
    for copy in copies[segments:]:
        copy.wait()
    live_ref[...] = jnp.full(live_ref.shape, count_ref[0])


def station_columns(pair_refs, hours, share):
    near = len(pair_refs)
    rows = share * hours * near
    lane = lax.broadcasted_iota(jnp.int32, (rows, hours * share), 1)
    row = lax.broadcasted_iota(jnp.int32, (rows, hours * share), 0)
    place = hours * near - 1 - row % (hours * near)
    owner = place % near
    slot = place // near * share + row // (near * hours)
    second = lax.axis_index("sta") % near == 1
    columns = []
    for side in range(2):
        mine, other = [jnp.broadcast_to(ref[side : side + 1], lane.shape) for ref in pair_refs]
        lists = [jnp.where(second, other, mine), jnp.where(second, mine, other)]
        value = jnp.where(owner == 1, lists[1], lists[0])
        columns.append(jnp.sum(jnp.where(lane == slot, value, 0), axis=1, keepdims=True))
    return columns


def cross_kernel(segments, share, mine_ref, other_ref, w_ref, o_ref, rows):
    early, stations, late, blocks, _ = w_ref.shape
    hours, depth = early * late, stations * blocks
    near = 2
    group, chunk, _ = o_ref.shape
    slots = group * share
    halves = chunk // (share * PARTS * PARTS * 2)
    column = lax.broadcasted_iota(jnp.int32, (slots, depth), 1)
    sides = []
    for station in station_columns((mine_ref, other_ref), hours, share):
        place = station % near * (stations // near) + station // near
        offset = column - place * blocks
        sides.append([(offset == r).astype(jnp.bfloat16) for r in range(blocks)])
    chosen = jnp.concatenate(sides[0] + sides[1], axis=0)
    picked = []
    for h in range(0, hours, 2):
        two = [w_ref[e // late, :, e % late].reshape(depth, LANES) for e in range(h, min(h + 2, hours))]
        two = jnp.concatenate(two, axis=1)
        two = jnp.dot(chosen, two, preferred_element_type=jnp.float32)
        picked += [two[:, e : e + LANES] for e in range(0, two.shape[1], LANES)]

    def part(side, h, g, j, c, x):
        first = (side * blocks + ((g * halves + j) * PARTS + x) * 2 + c) * slots
        return picked[h][first : first + slots]

    for j in range(halves):
        real = [None] * (PARTS * PARTS)
        imag = [None] * (PARTS * PARTS)
        for h in range(hours):
            for g in range(segments):
                left = [[part(0, h, g, j, c, x) for x in range(PARTS)] for c in range(2)]
                right = [[part(1, h, g, j, c, x) for x in range(PARTS)] for c in range(2)]
                for x in range(PARTS):
                    for y in range(PARTS):
                        re = left[0][x] * right[0][y] + left[1][x] * right[1][y]
                        im = left[0][x] * right[1][y] - left[1][x] * right[0][y]
                        n = x * PARTS + y
                        real[n] = re if real[n] is None else real[n] + re
                        imag[n] = im if imag[n] is None else imag[n] + im
        for n in range(PARTS * PARTS):
            for c, total in enumerate((real[n], imag[n])):
                for u in range(share):
                    row = ((u * PARTS * PARTS + n) * 2 + c) * halves + j
                    rows[pl.ds(row, group, stride=chunk), :] = total[u * group : (u + 1) * group]
    o_ref[...] = rows[...].reshape(o_ref.shape).astype(jnp.bfloat16)


def lag_kernel(live_ref, d_ref, first_ref, second_ref, o_ref, rows, lags_ref, sems):
    share, lags = o_ref.shape[2:]
    shards = lax.axis_size("tm") * 2
    period = lags // shards
    pieces = period // LANES
    lines = d_ref.shape[0] // (pieces * shards)
    total = lines * shards
    rows[...] = d_ref[...].astype(jnp.float32)
    daily = []
    for k in range(pieces):
        column = [rows[pl.ds(r * pieces + k, shards, stride=lines * pieces), :] for r in range(lines)]
        daily.append(jnp.concatenate(column, axis=0).astype(jnp.bfloat16))
    half = pieces // 2
    daily = jnp.concatenate([jnp.concatenate(daily[c * half : (c + 1) * half], axis=1) for c in range(2)], axis=0)
    run = period // 2
    middle = jnp.dot(daily, first_ref[:run], preferred_element_type=jnp.float32)
    re = (middle[:total, :period] - middle[total:, period:]).reshape(lines, shards, period)
    im = (middle[:total, period:] + middle[total:, :period]).reshape(lines, shards, period)
    turn = first_ref[run : run + 2 * shards].astype(jnp.float32)
    turn = turn[:shards] + turn[shards:]
    cos, sin = turn[None, :, :period], turn[None, :, period:]
    turned = jnp.concatenate(
        [
            (re * cos - im * sin).reshape(total, period).astype(jnp.bfloat16),
            (re * sin + im * cos).reshape(total, period).astype(jnp.bfloat16),
        ],
        axis=0,
    )
    live = live_ref[:1, :1] - lax.axis_index("tm") * share
    cuts = sems.shape[0]
    depth = total // cuts
    slot = lax.broadcasted_iota(jnp.int32, (depth, period), 0) % share
    copies = []
    for cut in range(cuts):
        joined = jnp.dot(second_ref[cut * depth : (cut + 1) * depth], turned, preferred_element_type=jnp.float32)
        joined = jnp.where(slot < live, joined, 0.0)
        base = cut * (lags // cuts)
        for a in range(shards // cuts):
            for n in range(PARTS * PARTS):
                first = (a * PARTS * PARTS + n) * share
                value = joined[first : first + share].astype(jnp.bfloat16)
                lags_ref[n // PARTS, n % PARTS, :, base + a * period : base + (a + 1) * period] = value
        window = (slice(None),) * 3 + (pl.ds(base, lags // cuts),)
        copies.append(pltpu.make_async_copy(lags_ref.at[window], o_ref.at[window], sems.at[cut]))
        copies[-1].start()
    for copy in copies:
        copy.wait()


def lag_tables(bins, shards, share):
    lags = 2 * bins
    period = lags // shards
    lines = share * PARTS * PARTS
    lane = np.arange(LANES)
    inner = lane % shards * (LANES // shards) + lane // shards
    k = (np.arange(0, bins // shards, LANES)[:, None] + inner).reshape(-1, 1)
    b = np.arange(period)[None, :]
    d = np.arange(shards)[:, None]

    def turns(angle):
        return np.concatenate([np.cos(angle), np.sin(angle)], axis=1)

    fine = turns(d * b * (2.0 * math.pi / lags)) * bins**-0.5
    high = fine.astype(jnp.bfloat16).astype(np.float64)
    first = np.concatenate([turns((k * b % period) * (2.0 * math.pi / period)), high, fine - high])
    a = np.arange(shards)[:, None] - bins // period
    turn = (a * d.T % shards) * (2.0 * math.pi / shards)
    same = np.eye(lines).reshape(share, PARTS * PARTS, lines).transpose(1, 0, 2)
    second = [np.einsum("ad,nur->anurd", table, same) for table in (np.cos(turn), -np.sin(turn))]
    second = np.concatenate([table.reshape(lines * shards, -1) for table in second], axis=1)
    return jnp.asarray(first, jnp.bfloat16), jnp.asarray(second, jnp.bfloat16)


def body(spectra, pair_blocks, block_count):
    _, _, segments, parts, _, bins = spectra.shape
    slots = pair_blocks.shape[1]
    hours, stations = lax.axis_size("tm"), lax.axis_size("sta")
    near = 2
    shards = hours * near
    share = slots // hours
    run = bins // shards
    halves = run // LANES
    chunk_in = segments * halves * 2 * parts
    chunk_out = share * parts * parts * 2 * halves

    early = 2 if hours % 2 == 0 else 1
    late = hours // early
    order = [
        (th * late + tl, z * near + core)
        for th in range(early)
        for core in range(near)
        for z in range(stations // near)
        for tl in range(late)
    ]

    def shard(t, s):
        return shards - 1 - (t * near + s % near)

    swap = [(s, s ^ 1) for s in range(stations)]
    pairs = pair_blocks[0].T
    other = lax.ppermute(pair_blocks, "sta", swap)[0].T

    owners = [shard(t, s) for t, s in order]
    first, second = lag_tables(bins, shards, share)
    white, mine, live, first, second = kernel_call(
        functools.partial(whiten_kernel, owners, shards, segments),
        (
            pltpu.VMEM((hours * stations, chunk_in, LANES), jnp.bfloat16),
            pltpu.VMEM((2, slots), jnp.int32),
            pltpu.VMEM((SLAB, LANES), jnp.int32),
            pltpu.VMEM(first.shape, first.dtype),
            pltpu.VMEM(second.shape, second.dtype),
        ),
        [HBM, HBM, pl.BlockSpec(memory_space=pltpu.SMEM), HBM, HBM],
        [
            pltpu.VMEM((segments * parts, 2, bins), jnp.bfloat16),
            pltpu.VMEM((shards, chunk_in, LANES), jnp.float32),
            pltpu.SemaphoreType.DMA((segments + 3,)),
        ],
    )(
        in_hbm(spectra.reshape(segments * parts, 2, bins)),
        in_hbm(pairs),
        block_count,
        in_hbm(first),
        in_hbm(second),
    )
    white, other = lax.optimization_barrier((white, other))
    groups = [[t * stations + s for t, s in order]]
    every = lax.all_to_all(white, MESH_AXES, 0, 0, tiled=True, axis_index_groups=groups)

    daily = kernel_call(
        functools.partial(cross_kernel, segments, share),
        pltpu.VMEM((shards, chunk_out, LANES), jnp.bfloat16),
        [VMEM] * 3,
        [pltpu.VMEM((shards * chunk_out, LANES), jnp.float32)],
    )(mine, other, every.reshape(early, stations, late, chunk_in, LANES))

    groups = [
        [t * stations + s + e for t in reversed(range(hours)) for e in reversed(range(near))]
        for s in range(0, stations, near)
    ]
    whole = lax.all_to_all(daily, MESH_AXES, 0, 0, tiled=True, axis_index_groups=groups)

    result = kernel_call(
        lag_kernel,
        jax.ShapeDtypeStruct((parts, parts, share, 2 * bins), jnp.bfloat16),
        [VMEM] * 4,
        [
            pltpu.VMEM((shards * chunk_out, LANES), jnp.float32),
            pltpu.VMEM((parts, parts, share, 2 * bins), jnp.bfloat16),
            pltpu.SemaphoreType.DMA((2,)),
        ],
        pl.BlockSpec(memory_space=pl.ANY),
    )(live, whole.reshape(shards * chunk_out, LANES), first, second)
    return result.transpose(2, 0, 1, 3).reshape(1, share, 1, 1, parts, parts, 2 * bins)


def solution(mesh):
    placed = (P("tm", "sta", None, None, None, None), P("sta", None, None), P("sta"))
    return jax.shard_map(
        body,
        mesh=mesh,
        in_specs=placed,
        out_specs=P("sta", "tm", None, None, None, None, None),
        check_vma=False,
    )
```

```python
import functools
import itertools
import math

import jax
import jax.numpy as jnp
import numpy as np
from jax import lax
from jax.experimental import pallas as pl
from jax.experimental.pallas import tpu as pltpu
from jax.sharding import PartitionSpec as P

SMOOTH = 64
LANES = 128
PARTS = 3
SLAB = 8

epsilon = 1e-05
MESH_AXES = ("tm", "sta")
VMEM = pl.BlockSpec(memory_space=pltpu.VMEM)
HBM = pl.BlockSpec(memory_space=pltpu.HBM)


def in_hbm(array):
    return pltpu.with_memory_space_constraint(array, pltpu.HBM)


def kernel_call(kernel, out_shape, in_specs, scratch, out_spec=VMEM):
    return pl.pallas_call(
        kernel,
        out_shape=out_shape,
        in_specs=in_specs,
        out_specs=jax.tree.map(lambda _: out_spec, out_shape),
        scratch_shapes=scratch,
        compiler_params=pltpu.CompilerParams(vmem_limit_bytes=40 * 1024 * 1024),
    )


def whiten_kernel(
    owners, shards, segments, spectra_ref, pairs_ref, count_ref, *refs
):
    first_ref, second_ref, o_ref, mine_ref, live_ref, first_held, second_held, x_ref, rows, sems = refs
    bins = x_ref.shape[2]
    tiles = bins // LANES
    moves = [(spectra_ref.at[pl.ds(g * PARTS, PARTS)], x_ref.at[pl.ds(g * PARTS, PARTS)]) for g in range(segments)]
    moves += [(pairs_ref, mine_ref), (first_ref, first_held), (second_ref, second_held)]
    copies = [pltpu.make_async_copy(*move, sems.at[n]) for n, move in enumerate(moves)]
    for copy in copies:
        copy.start()
    lane = lax.broadcasted_iota(jnp.int32, (SLAB, LANES), 1)
    even = lax.broadcasted_iota(jnp.int32, (SLAB, LANES), 0) % 2 == 0
    turn = [lane % shards == k for k in range(shards)]
    blank = jnp.zeros((SLAB, LANES), jnp.float32)
    apart = lax.broadcasted_iota(jnp.int32, (3 * LANES, LANES), 0) - LANES
    apart = apart - lax.broadcasted_iota(jnp.int32, (3 * LANES, LANES), 1)
    band = (jnp.abs(apart) <= SMOOTH).astype(jnp.bfloat16)
    values, blocks = [], []
    for g in range(segments):
        copies[g].wait()
        lines = [x_ref[g * PARTS + x].astype(jnp.float32) for x in range(PARTS)]
        lines = jnp.concatenate(lines + [jnp.zeros((SLAB - 2 * PARTS, bins), jnp.float32)], axis=0)
        value = [lines[:, v * LANES : (v + 1) * LANES] for v in range(tiles)]
        size = [blank]
        for v in range(tiles):
            square = value[v] * value[v]
            twin = jnp.where(even, pltpu.roll(square, SLAB - 1, 0), pltpu.roll(square, 1, 0))
            size.append(jnp.sqrt(square + twin))
        size.append(blank)
        values.append(value)
        blocks += [jnp.concatenate(size[v : v + 3], axis=1) for v in range(tiles)]
    stacked = jnp.concatenate(blocks, axis=0)
    high = stacked.astype(jnp.bfloat16)
    low = (stacked - high.astype(jnp.float32)).astype(jnp.bfloat16)
    window = jnp.dot(high, band, preferred_element_type=jnp.float32) + jnp.dot(
        low, band, preferred_element_type=jnp.float32
    )
    halves = tiles // shards
    for g in range(segments):
        for j in range(halves):
            moved = []
            for i in range(shards):
                v = j * shards + i
                place = lane + v * LANES
                count = jnp.minimum(place + SMOOTH, bins - 1) - jnp.maximum(place - SMOOTH, 0) + 1
                first = (g * tiles + v) * SLAB
                smoothed = window[first : first + SLAB] / count.astype(jnp.float32)
                white = values[g][v] / (smoothed + epsilon)
                moved.append(pltpu.roll(white, i, 1) if i else white)
            first = (g * halves + j) * 2 * PARTS
            for d in range(shards):
                mixed = moved[0]
                for i in range(1, shards):
                    mixed = jnp.where(turn[(d + i) % shards], moved[i], mixed)
                if d:
                    mixed = pltpu.roll(mixed, LANES - d, 1)
                rows[d, first : first + 2 * PARTS] = mixed[: 2 * PARTS]
    packed = rows[...].astype(jnp.bfloat16)
    lines = rows.shape[1]
    for device, classes in enumerate(owners):
        for e, d in enumerate(classes):
            o_ref[device, e * lines : (e + 1) * lines] = packed[d]
    for copy in copies[segments:]:
        copy.wait()
    live_ref[...] = jnp.full(live_ref.shape, count_ref[0])


def station_columns(pair_refs, hours, share):
    near = len(pair_refs)
    rows = share * hours * near
    lane = lax.broadcasted_iota(jnp.int32, (rows, hours * share), 1)
    row = lax.broadcasted_iota(jnp.int32, (rows, hours * share), 0)
    place = hours * near - 1 - row % (hours * near)
    owner = place % near
    slot = place // near * share + row // (near * hours)
    second = lax.axis_index("sta") % near == 1
    columns = []
    for side in range(2):
        mine, other = [jnp.broadcast_to(ref[side : side + 1], lane.shape) for ref in pair_refs]
        lists = [jnp.where(second, other, mine), jnp.where(second, mine, other)]
        value = jnp.where(owner == 1, lists[1], lists[0])
        columns.append(jnp.sum(jnp.where(lane == slot, value, 0), axis=1, keepdims=True))
    return columns


def station_place(station, stations, near):
    chips = stations // near
    return (near - 1 - station % near) * chips + (station // near + chips - chips // 2) % chips


def cross_kernel(segments, share, mine_ref, other_ref, w_ref, o_ref, rows):
    hours, stations, classes, blocks, _ = w_ref.shape
    depth = stations * blocks
    near = 2
    group, chunk, _ = o_ref.shape
    slots = group * share
    halves = chunk // (classes * share * PARTS * PARTS * 2)
    column = lax.broadcasted_iota(jnp.int32, (slots, depth), 1)
    sides = []
    for station in station_columns((mine_ref, other_ref), group // near, share):
        place = station_place(station, stations, near)
        offset = column - place * blocks
        sides.append([(offset == r).astype(jnp.bfloat16) for r in range(blocks)])
    chosen = jnp.concatenate(sides[0] + sides[1], axis=0)
    columns = [w_ref[h, :, e].reshape(depth, LANES) for h in range(hours) for e in range(classes)]
    picked = []
    for m in range(0, len(columns), 2):
        two = jnp.concatenate(columns[m : m + 2], axis=1)
        two = jnp.dot(chosen, two, preferred_element_type=jnp.float32)
        picked += [two[:, n : n + LANES] for n in range(0, two.shape[1], LANES)]

    def part(side, h, e, g, j, c, x):
        first = (side * blocks + ((g * halves + j) * PARTS + x) * 2 + c) * slots
        return picked[h * classes + e][first : first + slots]

    for e, j in itertools.product(range(classes), range(halves)):
        real = [None] * (PARTS * PARTS)
        imag = [None] * (PARTS * PARTS)
        for h in range(hours):
            for g in range(segments):
                left = [[part(0, h, e, g, j, c, x) for x in range(PARTS)] for c in range(2)]
                right = [[part(1, h, e, g, j, c, x) for x in range(PARTS)] for c in range(2)]
                for x in range(PARTS):
                    for y in range(PARTS):
                        re = left[0][x] * right[0][y] + left[1][x] * right[1][y]
                        im = left[0][x] * right[1][y] - left[1][x] * right[0][y]
                        n = x * PARTS + y
                        real[n] = re if real[n] is None else real[n] + re
                        imag[n] = im if imag[n] is None else imag[n] + im
        for n in range(PARTS * PARTS):
            for c, total in enumerate((real[n], imag[n])):
                for u in range(share):
                    row = (((e * share + u) * PARTS * PARTS + n) * 2 + c) * halves + j
                    rows[pl.ds(row, group, stride=chunk), :] = total[u * group : (u + 1) * group]
    o_ref[...] = rows[...].reshape(o_ref.shape).astype(jnp.bfloat16)


def lag_kernel(live_ref, d_ref, first_ref, second_ref, o_ref, rows, lags_ref, sems):
    share, lags = o_ref.shape[2:]
    shards = lax.axis_size("tm") * 2
    period = lags // shards
    pieces = period // LANES
    lines = d_ref.shape[1] // (pieces * shards)
    total = lines * shards
    rows[...] = sum(d_ref[h].astype(jnp.float32) for h in range(d_ref.shape[0]))
    daily = []
    for k in range(pieces):
        column = [rows[pl.ds(r * pieces + k, shards, stride=lines * pieces), :] for r in range(lines)]
        daily.append(jnp.concatenate(column, axis=0).astype(jnp.bfloat16))
    half = pieces // 2
    daily = jnp.concatenate([jnp.concatenate(daily[c * half : (c + 1) * half], axis=1) for c in range(2)], axis=0)
    run = period // 2
    middle = jnp.dot(daily, first_ref[:run], preferred_element_type=jnp.float32)
    re = (middle[:total, :period] - middle[total:, period:]).reshape(lines, shards, period)
    im = (middle[:total, period:] + middle[total:, :period]).reshape(lines, shards, period)
    turn = first_ref[run : run + 2 * shards].astype(jnp.float32)
    turn = turn[:shards] + turn[shards:]
    cos, sin = turn[None, :, :period], turn[None, :, period:]
    turned = jnp.concatenate(
        [
            (re * cos - im * sin).reshape(total, period).astype(jnp.bfloat16),
            (re * sin + im * cos).reshape(total, period).astype(jnp.bfloat16),
        ],
        axis=0,
    )
    live = live_ref[:1, :1] - lax.axis_index("tm") * share
    cuts = sems.shape[0]
    depth = total // cuts
    slot = lax.broadcasted_iota(jnp.int32, (depth, period), 0) % share
    copies = []
    for cut in range(cuts):
        joined = jnp.dot(second_ref[cut * depth : (cut + 1) * depth], turned, preferred_element_type=jnp.float32)
        joined = jnp.where(slot < live, joined, 0.0)
        base = cut * (lags // cuts)
        for a in range(shards // cuts):
            for n in range(PARTS * PARTS):
                first = (a * PARTS * PARTS + n) * share
                value = joined[first : first + share].astype(jnp.bfloat16)
                lags_ref[n // PARTS, n % PARTS, :, base + a * period : base + (a + 1) * period] = value
        window = (slice(None),) * 3 + (pl.ds(base, lags // cuts),)
        copies.append(pltpu.make_async_copy(lags_ref.at[window], o_ref.at[window], sems.at[cut]))
        copies[-1].start()
    for copy in copies:
        copy.wait()


def lag_tables(bins, shards, share):
    lags = 2 * bins
    period = lags // shards
    lines = share * PARTS * PARTS
    lane = np.arange(LANES)
    inner = lane % shards * (LANES // shards) + lane // shards
    k = (np.arange(0, bins // shards, LANES)[:, None] + inner).reshape(-1, 1)
    b = np.arange(period)[None, :]
    d = np.arange(shards)[:, None]

    def turns(angle):
        return np.concatenate([np.cos(angle), np.sin(angle)], axis=1)

    fine = turns(d * b * (2.0 * math.pi / lags)) * bins**-0.5
    high = fine.astype(jnp.bfloat16).astype(np.float64)
    first = np.concatenate([turns((k * b % period) * (2.0 * math.pi / period)), high, fine - high])
    a = np.arange(shards)[:, None] - bins // period
    turn = (a * d.T % shards) * (2.0 * math.pi / shards)
    same = np.eye(lines).reshape(share, PARTS * PARTS, lines).transpose(1, 0, 2)
    second = [np.einsum("ad,nur->anurd", table, same) for table in (np.cos(turn), -np.sin(turn))]
    second = np.concatenate([table.reshape(lines * shards, -1) for table in second], axis=1)
    return jnp.asarray(first, jnp.bfloat16), jnp.asarray(second, jnp.bfloat16)


def body(spectra, pair_blocks, block_count):
    _, _, segments, parts, _, bins = spectra.shape
    slots = pair_blocks.shape[1]
    hours, stations = lax.axis_size("tm"), lax.axis_size("sta")
    near = 2
    shards = hours * near
    share = slots // hours
    run = bins // shards
    halves = run // LANES
    chunk_in = segments * halves * 2 * parts
    chunk_out = share * parts * parts * 2 * halves

    early = 2 if hours % 2 == 0 else 1
    late = hours // early
    chips = stations // near
    order = [
        (t, (z + chips // 2) % chips * near + core)
        for t in reversed(range(late))
        for core in reversed(range(near))
        for z in range(chips)
    ]

    swap = [(s, s ^ 1) for s in range(stations)]
    pairs = pair_blocks[0].T
    other = lax.ppermute(pair_blocks, "sta", swap)[0].T

    pieces = late * near
    owners = [
        [(pieces - 1 - (t * near + s % near)) * early + e for e in range(early)] for t, s in order
    ]
    first, second = lag_tables(bins, shards, share)
    white, mine, live, first, second = kernel_call(
        functools.partial(whiten_kernel, owners, shards, segments),
        (
            pltpu.VMEM((late * stations, early * chunk_in, LANES), jnp.bfloat16),
            pltpu.VMEM((2, slots), jnp.int32),
            pltpu.VMEM((SLAB, LANES), jnp.int32),
            pltpu.VMEM(first.shape, first.dtype),
            pltpu.VMEM(second.shape, second.dtype),
        ),
        [HBM, HBM, pl.BlockSpec(memory_space=pltpu.SMEM), HBM, HBM],
        [
            pltpu.VMEM((segments * parts, 2, bins), jnp.bfloat16),
            pltpu.VMEM((shards, chunk_in, LANES), jnp.float32),
            pltpu.SemaphoreType.DMA((segments + 3,)),
        ],
    )(
        in_hbm(spectra.reshape(segments * parts, 2, bins)),
        in_hbm(pairs),
        block_count,
        in_hbm(first),
        in_hbm(second),
    )
    white, other = lax.optimization_barrier((white, other))
    groups = [[(h * late + t) * stations + s for t, s in order] for h in range(early)]
    every = lax.all_to_all(white, MESH_AXES, 0, 0, tiled=True, axis_index_groups=groups)

    daily = kernel_call(
        functools.partial(cross_kernel, segments, share),
        pltpu.VMEM((shards, early * chunk_out, LANES), jnp.bfloat16),
        [VMEM] * 3,
        [pltpu.VMEM((shards * early * chunk_out, LANES), jnp.float32)],
    )(mine, other, every.reshape(late, stations, early, chunk_in, LANES))

    groups = [
        [t * stations + s + e for t in reversed(range(hours)) for e in reversed(range(near))]
        for s in range(0, stations, near)
    ]
    whole = lax.all_to_all(daily, MESH_AXES, 0, 0, tiled=True, axis_index_groups=groups)

    result = kernel_call(
        lag_kernel,
        jax.ShapeDtypeStruct((parts, parts, share, 2 * bins), jnp.bfloat16),
        [VMEM] * 4,
        [
            pltpu.VMEM((shards * chunk_out, LANES), jnp.float32),
            pltpu.VMEM((parts, parts, share, 2 * bins), jnp.bfloat16),
            pltpu.SemaphoreType.DMA((2,)),
        ],
        pl.BlockSpec(memory_space=pl.ANY),
    )(live, whole.reshape(early, shards * chunk_out, LANES), first, second)
    return result.transpose(2, 0, 1, 3).reshape(1, share, 1, 1, parts, parts, 2 * bins)


def solution(mesh):
    placed = (P("tm", "sta", None, None, None, None), P("sta", None, None), P("sta"))
    return jax.shard_map(
        body,
        mesh=mesh,
        in_specs=placed,
        out_specs=P("sta", "tm", None, None, None, None, None),
        check_vma=False,
    )
```

```python
import functools
import math

import jax
import jax.numpy as jnp
import numpy as np
from jax import lax
from jax.experimental import pallas as pl
from jax.experimental.pallas import tpu as pltpu
from jax.sharding import PartitionSpec as P

SMOOTH = 64
LANES = 128
PARTS = 3
SLAB = 8

CORES = 2

epsilon = 1e-05
MESH_AXES = ("tm", "sta")
VMEM = pl.BlockSpec(memory_space=pltpu.VMEM)
HBM = pl.BlockSpec(memory_space=pltpu.HBM)


def in_hbm(array):
    return pltpu.with_memory_space_constraint(array, pltpu.HBM)


def kernel_call(kernel, out_shape, in_specs, scratch, out_spec=VMEM):
    return pl.pallas_call(
        kernel,
        out_shape=out_shape,
        in_specs=in_specs,
        out_specs=jax.tree.map(lambda _: out_spec, out_shape),
        scratch_shapes=scratch,
        compiler_params=pltpu.CompilerParams(vmem_limit_bytes=40 * 1024 * 1024),
    )


def whiten_kernel(
    classes, shards, segments, spectra_ref, pairs_ref, count_ref, *refs
):
    first_ref, second_ref, o_ref, first_held, second_held, x_ref, rows, pairs, sems = refs
    bins = x_ref.shape[2]
    tiles = bins // LANES
    moves = [(spectra_ref.at[pl.ds(g * PARTS, PARTS)], x_ref.at[pl.ds(g * PARTS, PARTS)]) for g in range(segments)]
    moves += [(pairs_ref, pairs), (first_ref, first_held), (second_ref, second_held)]
    copies = [pltpu.make_async_copy(*move, sems.at[n]) for n, move in enumerate(moves)]
    for copy in copies:
        copy.start()
    lane = lax.broadcasted_iota(jnp.int32, (SLAB, LANES), 1)
    even = lax.broadcasted_iota(jnp.int32, (SLAB, LANES), 0) % 2 == 0
    turn = [lane % shards == k for k in range(shards)]
    blank = jnp.zeros((SLAB, LANES), jnp.float32)
    apart = lax.broadcasted_iota(jnp.int32, (3 * LANES, LANES), 0) - LANES
    apart = apart - lax.broadcasted_iota(jnp.int32, (3 * LANES, LANES), 1)
    band = (jnp.abs(apart) <= SMOOTH).astype(jnp.bfloat16)
    values, blocks = [], []
    for g in range(segments):
        copies[g].wait()
        lines = [x_ref[g * PARTS + x].astype(jnp.float32) for x in range(PARTS)]
        lines = jnp.concatenate(lines + [jnp.zeros((SLAB - 2 * PARTS, bins), jnp.float32)], axis=0)
        value = [lines[:, v * LANES : (v + 1) * LANES] for v in range(tiles)]
        size = [blank]
        for v in range(tiles):
            square = value[v] * value[v]
            twin = jnp.where(even, pltpu.roll(square, SLAB - 1, 0), pltpu.roll(square, 1, 0))
            size.append(jnp.sqrt(square + twin))
        size.append(blank)
        values.append(value)
        blocks += [jnp.concatenate(size[v : v + 3], axis=1) for v in range(tiles)]
    stacked = jnp.concatenate(blocks, axis=0)
    high = stacked.astype(jnp.bfloat16)
    low = (stacked - high.astype(jnp.float32)).astype(jnp.bfloat16)
    window = jnp.dot(high, band, preferred_element_type=jnp.float32) + jnp.dot(
        low, band, preferred_element_type=jnp.float32
    )
    halves = tiles // shards
    for g in range(segments):
        for j in range(halves):
            moved = []
            for i in range(shards):
                v = j * shards + i
                place = lane + v * LANES
                count = jnp.minimum(place + SMOOTH, bins - 1) - jnp.maximum(place - SMOOTH, 0) + 1
                first = (g * tiles + v) * SLAB
                smoothed = window[first : first + SLAB] / count.astype(jnp.float32)
                white = values[g][v] / (smoothed + epsilon)
                moved.append(pltpu.roll(white, i, 1) if i else white)
            first = (g * halves + j) * 2 * PARTS
            for d in range(shards):
                mixed = moved[0]
                for i in range(1, shards):
                    mixed = jnp.where(turn[(d + i) % shards], moved[i], mixed)
                if d:
                    mixed = pltpu.roll(mixed, LANES - d, 1)
                rows[d, first : first + 2 * PARTS] = mixed[: 2 * PARTS]
    packed = rows[...].astype(jnp.bfloat16)
    for copy in copies[segments:]:
        copy.wait()
    slots = pairs.shape[1]
    lists = jnp.concatenate([pairs[...].astype(jnp.float32), jnp.zeros((2, LANES - slots), jnp.float32)], axis=1)
    counts = jnp.full((SLAB - 2, LANES), count_ref[0].astype(jnp.float32))
    lists = jnp.concatenate([lists, counts], axis=0).astype(jnp.bfloat16)
    lines = rows.shape[1]
    for place, d in enumerate(classes):
        o_ref[place, :lines] = packed[d]
        o_ref[place, lines:] = lists


def station_columns(lists, hours, share):
    near = len(lists)
    group = hours * near
    rows = share * group
    lane = lax.broadcasted_iota(jnp.int32, (rows, LANES), 1)
    row = lax.broadcasted_iota(jnp.int32, (rows, LANES), 0)
    place = group - 1 - row % group
    owner = place // (hours * CORES) * CORES + place % CORES
    slot = place // CORES % hours * share + row // group
    columns = []
    for side in range(3):
        value = jnp.broadcast_to(lists[0][side : side + 1], lane.shape)
        for n in range(1, near):
            value = jnp.where(owner == n, lists[n][side : side + 1], value)
        columns.append(jnp.sum(jnp.where(lane == slot, value, 0.0), axis=1, keepdims=True).astype(jnp.int32))
    live = slot[:, :1] < columns[2]
    return [jnp.where(live, column, -1) for column in columns[:2]]


def first_order(hours, stations):
    chips = stations // CORES
    middle = chips // 2
    along = [*range(middle, -1, -1), *range(middle + 1, chips)]
    return [(t, z * CORES + core) for t in reversed(range(hours)) for z in along for core in reversed(range(CORES))]


def second_order(hours, near):
    order = [(t, z * CORES + core) for z in range(near // CORES) for t in range(hours) for core in range(CORES)]
    return order[::-1]


def cross_kernel(segments, share, near, w_ref, o_ref, rows):
    hours, stations, lines, _ = w_ref.shape
    blocks = lines - SLAB
    depth = stations * blocks
    group, chunk, _ = o_ref.shape
    slots = group * share
    halves = chunk // (share * PARTS * PARTS * 2)
    place_of = [station for _, station in first_order(1, stations)]
    place_of = [place_of.index(station) for station in range(stations)]
    cluster = lax.axis_index("sta") // near
    lists = []
    for n in range(near):
        place = 0
        for m in range(stations // near):
            place = jnp.where(cluster == m, place_of[m * near + n], place)
        lists.append(w_ref[0, pl.ds(place, 1), blocks:].reshape(SLAB, LANES).astype(jnp.float32))
    column = lax.broadcasted_iota(jnp.int32, (slots, depth), 1)
    sides = []
    for station in station_columns(lists, group // near, share):
        first = jnp.full(station.shape, depth)
        for m in range(stations):
            first = jnp.where(station == m, place_of[m] * blocks, first)
        offset = column - first
        sides.append([(offset == r).astype(jnp.bfloat16) for r in range(blocks)])
    chosen = jnp.concatenate(sides[0] + sides[1], axis=0)
    columns = [w_ref[h, :, :blocks].reshape(depth, LANES) for h in range(hours)]
    picked = []
    for m in range(0, len(columns), 2):
        two = jnp.concatenate(columns[m : m + 2], axis=1)
        two = jnp.dot(chosen, two, preferred_element_type=jnp.float32)
        picked += [two[:, n : n + LANES] for n in range(0, two.shape[1], LANES)]

    def part(side, h, g, j, c, x):
        first = (side * blocks + ((g * halves + j) * PARTS + x) * 2 + c) * slots
        return picked[h][first : first + slots]

    for j in range(halves):
        real = [None] * (PARTS * PARTS)
        imag = [None] * (PARTS * PARTS)
        for h in range(hours):
            for g in range(segments):
                left = [[part(0, h, g, j, c, x) for x in range(PARTS)] for c in range(2)]
                right = [[part(1, h, g, j, c, x) for x in range(PARTS)] for c in range(2)]
                for x in range(PARTS):
                    for y in range(PARTS):
                        re = left[0][x] * right[0][y] + left[1][x] * right[1][y]
                        im = left[0][x] * right[1][y] - left[1][x] * right[0][y]
                        n = x * PARTS + y
                        real[n] = re if real[n] is None else real[n] + re
                        imag[n] = im if imag[n] is None else imag[n] + im
        for n in range(PARTS * PARTS):
            for c, total in enumerate((real[n], imag[n])):
                for u in range(share):
                    row = ((u * PARTS * PARTS + n) * 2 + c) * halves + j
                    rows[pl.ds(row, group, stride=chunk), :] = total[u * group : (u + 1) * group]
    o_ref[...] = rows[...].reshape(o_ref.shape).astype(jnp.bfloat16)


def lag_kernel(shards, d_ref, first_ref, second_ref, o_ref, rows, lags_ref, sems):
    share, lags = o_ref.shape[2:]
    period = lags // shards
    pieces = period // LANES
    chips, hours, depth, _ = d_ref.shape
    total = chips * depth // pieces
    lines = total // shards
    for z in range(chips):
        rows[z * depth : (z + 1) * depth] = sum(d_ref[z, h].astype(jnp.float32) for h in range(hours))
    daily = []
    for k in range(pieces):
        column = [rows[pl.ds(r * pieces + k, shards, stride=lines * pieces), :] for r in range(lines)]
        daily.append(jnp.concatenate(column, axis=0).astype(jnp.bfloat16))
    half = pieces // 2
    daily = jnp.concatenate([jnp.concatenate(daily[c * half : (c + 1) * half], axis=1) for c in range(2)], axis=0)
    run = period // 2
    middle = jnp.dot(daily, first_ref[:run], preferred_element_type=jnp.float32)
    re = (middle[:total, :period] - middle[total:, period:]).reshape(lines, shards, period)
    im = (middle[:total, period:] + middle[total:, :period]).reshape(lines, shards, period)
    turn = first_ref[run : run + 2 * shards].astype(jnp.float32)
    turn = turn[:shards] + turn[shards:]
    cos, sin = turn[None, :, :period], turn[None, :, period:]
    turned = jnp.concatenate(
        [
            (re * cos - im * sin).reshape(total, period).astype(jnp.bfloat16),
            (re * sin + im * cos).reshape(total, period).astype(jnp.bfloat16),
        ],
        axis=0,
    )
    cuts = sems.shape[0]
    depth = total // cuts
    copies = []
    for cut in range(cuts):
        joined = jnp.dot(second_ref[cut * depth : (cut + 1) * depth], turned, preferred_element_type=jnp.float32)
        base = cut * (lags // cuts)
        for a in range(shards // cuts):
            for n in range(PARTS * PARTS):
                first = (a * PARTS * PARTS + n) * share
                value = joined[first : first + share].astype(jnp.bfloat16)
                lags_ref[n // PARTS, n % PARTS, :, base + a * period : base + (a + 1) * period] = value
        window = (slice(None),) * 3 + (pl.ds(base, lags // cuts),)
        copies.append(pltpu.make_async_copy(lags_ref.at[window], o_ref.at[window], sems.at[cut]))
        copies[-1].start()
    for copy in copies:
        copy.wait()


def lag_tables(bins, shards, share):
    lags = 2 * bins
    period = lags // shards
    lines = share * PARTS * PARTS
    lane = np.arange(LANES)
    inner = lane % shards * (LANES // shards) + lane // shards
    k = (np.arange(0, bins // shards, LANES)[:, None] + inner).reshape(-1, 1)
    b = np.arange(period)[None, :]
    d = np.arange(shards)[:, None]

    def turns(angle):
        return np.concatenate([np.cos(angle), np.sin(angle)], axis=1)

    fine = turns(d * b * (2.0 * math.pi / lags)) * bins**-0.5
    high = fine.astype(jnp.bfloat16).astype(np.float64)
    first = np.concatenate([turns((k * b % period) * (2.0 * math.pi / period)), high, fine - high])
    a = np.arange(shards)[:, None] - bins // period
    turn = (a * d.T % shards) * (2.0 * math.pi / shards)
    same = np.eye(lines).reshape(share, PARTS * PARTS, lines).transpose(1, 0, 2)
    second = [np.einsum("ad,nur->anurd", table, same) for table in (np.cos(turn), -np.sin(turn))]
    second = np.concatenate([table.reshape(lines * shards, -1) for table in second], axis=1)
    return jnp.asarray(first, jnp.bfloat16), jnp.asarray(second, jnp.bfloat16)


def body(spectra, pair_blocks, block_count):
    _, _, segments, parts, _, bins = spectra.shape
    slots = pair_blocks.shape[1]
    hours, stations = lax.axis_size("tm"), lax.axis_size("sta")
    near = 2 * CORES if stations % (2 * CORES) == 0 else CORES
    early = 2 if hours % 2 == 0 else 1
    late = hours // early
    shards = late * near
    share = slots // hours
    run = bins // shards
    halves = run // LANES
    chunk_in = segments * halves * 2 * parts
    chunk_out = share * parts * parts * 2 * halves
    order = first_order(late, stations)
    shard_of = second_order(late, near)
    classes = [shard_of.index((t, s % near)) for t, s in order]
    first, second = lag_tables(bins, shards, share)
    white, first, second = kernel_call(
        functools.partial(whiten_kernel, classes, shards, segments),
        (
            pltpu.VMEM((late * stations, chunk_in + SLAB, LANES), jnp.bfloat16),
            pltpu.VMEM(first.shape, first.dtype),
            pltpu.VMEM(second.shape, second.dtype),
        ),
        [HBM, HBM, pl.BlockSpec(memory_space=pltpu.SMEM), HBM, HBM],
        [
            pltpu.VMEM((segments * parts, 2, bins), jnp.bfloat16),
            pltpu.VMEM((shards, chunk_in, LANES), jnp.float32),
            pltpu.VMEM((2, slots), jnp.int32),
            pltpu.SemaphoreType.DMA((segments + 3,)),
        ],
    )(
        in_hbm(spectra.reshape(segments * parts, 2, bins)),
        in_hbm(pair_blocks[0].T),
        block_count,
        in_hbm(first),
        in_hbm(second),
    )
    groups = [[(h * late + t) * stations + s for t, s in order] for h in range(early)]
    every = lax.all_to_all(white, MESH_AXES, 0, 0, tiled=True, axis_index_groups=groups)

    daily = kernel_call(
        functools.partial(cross_kernel, segments, share, near),
        pltpu.VMEM((hours * near, chunk_out, LANES), jnp.bfloat16),
        [VMEM],
        [pltpu.VMEM((hours * near * chunk_out, LANES), jnp.float32)],
    )(every.reshape(late, stations, chunk_in + SLAB, LANES))

    order = second_order(hours, near)
    groups = [[t * stations + s + m for t, m in order] for s in range(0, stations, near)]
    whole = lax.all_to_all(daily, MESH_AXES, 0, 0, tiled=True, axis_index_groups=groups)

    result = kernel_call(
        functools.partial(lag_kernel, shards),
        jax.ShapeDtypeStruct((parts, parts, share, 2 * bins), jnp.bfloat16),
        [VMEM] * 3,
        [
            pltpu.VMEM((shards * chunk_out, LANES), jnp.float32),
            pltpu.VMEM((parts, parts, share, 2 * bins), jnp.bfloat16),
            pltpu.SemaphoreType.DMA((2,)),
        ],
        pl.BlockSpec(memory_space=pl.ANY),
    )(whole.reshape(near // CORES, early, late * CORES * chunk_out, LANES), first, second)
    return result.transpose(2, 0, 1, 3).reshape(1, share, 1, 1, parts, parts, 2 * bins)


def solution(mesh):
    placed = (P("tm", "sta", None, None, None, None), P("sta", None, None), P("sta"))
    return jax.shard_map(
        body,
        mesh=mesh,
        in_specs=placed,
        out_specs=P("sta", "tm", None, None, None, None, None),
        check_vma=False,
    )
```

```python
import functools
import math

import jax
import jax.numpy as jnp
import numpy as np
from jax import lax
from jax.experimental import pallas as pl
from jax.experimental.pallas import tpu as pltpu
from jax.sharding import PartitionSpec as P

SMOOTH = 64
LANES = 128
PARTS = 3
SLAB = 8

CORES = 2

epsilon = 1e-05
MESH_AXES = ("tm", "sta")
VMEM = pl.BlockSpec(memory_space=pltpu.VMEM)


placed = pltpu.with_memory_space_constraint


def kernel_call(kernel, out_shape, in_specs, scratch, out_spec=VMEM, weight=1):
    return pl.pallas_call(
        kernel,
        out_shape=out_shape,
        in_specs=in_specs,
        out_specs=jax.tree.map(lambda _: out_spec, out_shape),
        scratch_shapes=scratch,
        cost_estimate=pl.CostEstimate(flops=weight * 10**9, bytes_accessed=weight * 4 * 10**6, transcendentals=0),
        compiler_params=pltpu.CompilerParams(vmem_limit_bytes=40 * 1024 * 1024),
    )


def band_kernel(o_ref):
    apart = lax.broadcasted_iota(jnp.int32, (3 * LANES, LANES), 0) - LANES
    apart = apart - lax.broadcasted_iota(jnp.int32, (3 * LANES, LANES), 1)
    o_ref[...] = (jnp.abs(apart) <= SMOOTH).astype(jnp.bfloat16)


def whiten_kernel(
    classes, shards, segments, x_ref, pairs_ref, count_ref, band_ref, o_ref, rows, pairs, sem
):
    pairs_copy = pltpu.make_async_copy(pairs_ref, pairs, sem)
    pairs_copy.start()
    bins = x_ref.shape[2]
    tiles = bins // LANES
    lane = lax.broadcasted_iota(jnp.int32, (SLAB, LANES), 1)
    even = lax.broadcasted_iota(jnp.int32, (SLAB, LANES), 0) % 2 == 0
    turn = [lane % shards == k for k in range(shards)]
    blank = jnp.zeros((SLAB, LANES), jnp.float32)
    band = band_ref[...]
    values, blocks = [], []
    for g in range(segments):
        lines = [x_ref[g * PARTS + x].astype(jnp.float32) for x in range(PARTS)]
        lines = jnp.concatenate(lines + [jnp.zeros((SLAB - 2 * PARTS, bins), jnp.float32)], axis=0)
        value = [lines[:, v * LANES : (v + 1) * LANES] for v in range(tiles)]
        size = [blank]
        for v in range(tiles):
            square = value[v] * value[v]
            twin = jnp.where(even, pltpu.roll(square, SLAB - 1, 0), pltpu.roll(square, 1, 0))
            size.append(jnp.sqrt(square + twin))
        size.append(blank)
        values.append(value)
        blocks += [jnp.concatenate(size[v : v + 3], axis=1) for v in range(tiles)]
    stacked = jnp.concatenate(blocks, axis=0)
    high = stacked.astype(jnp.bfloat16)
    low = (stacked - high.astype(jnp.float32)).astype(jnp.bfloat16)
    window = jnp.dot(high, band, preferred_element_type=jnp.float32) + jnp.dot(
        low, band, preferred_element_type=jnp.float32
    )
    halves = tiles // shards
    for g in range(segments):
        for j in range(halves):
            moved = []
            for i in range(shards):
                v = j * shards + i
                place = lane + v * LANES
                count = jnp.minimum(place + SMOOTH, bins - 1) - jnp.maximum(place - SMOOTH, 0) + 1
                first = (g * tiles + v) * SLAB
                smoothed = window[first : first + SLAB] / count.astype(jnp.float32)
                white = values[g][v] / (smoothed + epsilon)
                moved.append(pltpu.roll(white, i, 1) if i else white)
            first = (g * halves + j) * 2 * PARTS
            for d in range(shards):
                mixed = moved[0]
                for i in range(1, shards):
                    mixed = jnp.where(turn[(d + i) % shards], moved[i], mixed)
                if d:
                    mixed = pltpu.roll(mixed, LANES - d, 1)
                rows[d, first : first + 2 * PARTS] = mixed[: 2 * PARTS]
    packed = rows[...].astype(jnp.bfloat16)
    pairs_copy.wait()
    slots = pairs.shape[1]
    lists = jnp.concatenate([pairs[...].astype(jnp.float32), jnp.zeros((2, LANES - slots), jnp.float32)], axis=1)
    counts = jnp.full((SLAB - 2, LANES), count_ref[0].astype(jnp.float32))
    lists = jnp.concatenate([lists, counts], axis=0).astype(jnp.bfloat16)
    lines = rows.shape[1]
    for place, d in enumerate(classes):
        o_ref[place, :lines] = packed[d]
        o_ref[place, lines:] = lists


def station_columns(lists, hours, share):
    near = len(lists)
    group = hours * near
    rows = share * group
    lane = lax.broadcasted_iota(jnp.int32, (rows, LANES), 1)
    row = lax.broadcasted_iota(jnp.int32, (rows, LANES), 0)
    place = group - 1 - row % group
    owner = place // hours % (near // CORES) * CORES + place // (hours * (near // CORES))
    slot = place % hours * share + row // group
    columns = []
    for side in range(3):
        value = jnp.broadcast_to(lists[0][side : side + 1], lane.shape)
        for n in range(1, near):
            value = jnp.where(owner == n, lists[n][side : side + 1], value)
        columns.append(jnp.sum(jnp.where(lane == slot, value, 0.0), axis=1, keepdims=True).astype(jnp.int32))
    live = slot[:, :1] < columns[2]
    return [jnp.where(live, column, -1) for column in columns[:2]]


def first_order(hours, stations):
    chips = stations // CORES
    middle = chips // 2
    along = [*range(middle, -1, -1), *range(middle + 1, chips)]
    return [(t, z * CORES + core) for t in reversed(range(hours)) for z in along for core in reversed(range(CORES))]


def second_order(hours, near):
    order = [(t, z * CORES + core) for core in range(CORES) for z in range(near // CORES) for t in range(hours)]
    return order[::-1]


def cross_kernel(segments, share, near, w_ref, o_ref, rows):
    hours, stations, lines, _ = w_ref.shape
    blocks = lines - SLAB
    depth = stations * blocks
    group, chunk, _ = o_ref.shape
    slots = group * share
    halves = chunk // (share * PARTS * PARTS * 2)
    place_of = [station for _, station in first_order(1, stations)]
    place_of = [place_of.index(station) for station in range(stations)]
    cluster = lax.axis_index("sta") // near
    lists = []
    for n in range(near):
        place = 0
        for m in range(stations // near):
            place = jnp.where(cluster == m, place_of[m * near + n], place)
        lists.append(w_ref[0, pl.ds(place, 1), blocks:].reshape(SLAB, LANES).astype(jnp.float32))
    column = lax.broadcasted_iota(jnp.int32, (slots, depth), 1)
    sides = []
    for station in station_columns(lists, group // near, share):
        first = jnp.full(station.shape, depth)
        for m in range(stations):
            first = jnp.where(station == m, place_of[m] * blocks, first)
        offset = column - first
        sides.append([(offset == r).astype(jnp.bfloat16) for r in range(blocks)])
    chosen = jnp.concatenate(sides[0] + sides[1], axis=0)
    columns = [w_ref[h, :, :blocks].reshape(depth, LANES) for h in range(hours)]
    picked = []
    for m in range(0, len(columns), 2):
        two = jnp.concatenate(columns[m : m + 2], axis=1)
        two = jnp.dot(chosen, two, preferred_element_type=jnp.float32)
        picked += [two[:, n : n + LANES] for n in range(0, two.shape[1], LANES)]

    def part(side, h, g, j, c, x):
        first = (side * blocks + ((g * halves + j) * PARTS + x) * 2 + c) * slots
        return picked[h][first : first + slots]

    for j in range(halves):
        real = [None] * (PARTS * PARTS)
        imag = [None] * (PARTS * PARTS)
        for h in range(hours):
            for g in range(segments):
                left = [[part(0, h, g, j, c, x) for x in range(PARTS)] for c in range(2)]
                right = [[part(1, h, g, j, c, x) for x in range(PARTS)] for c in range(2)]
                for x in range(PARTS):
                    for y in range(PARTS):
                        re = left[0][x] * right[0][y] + left[1][x] * right[1][y]
                        im = left[0][x] * right[1][y] - left[1][x] * right[0][y]
                        n = x * PARTS + y
                        real[n] = re if real[n] is None else real[n] + re
                        imag[n] = im if imag[n] is None else imag[n] + im
        for n in range(PARTS * PARTS):
            for c, total in enumerate((real[n], imag[n])):
                for u in range(share):
                    row = ((u * PARTS * PARTS + n) * 2 + c) * halves + j
                    rows[pl.ds(row, group, stride=chunk), :] = total[u * group : (u + 1) * group]
    o_ref[...] = rows[...].reshape(o_ref.shape).astype(jnp.bfloat16)


def lag_kernel(shards, d_ref, first_ref, second_ref, o_ref, rows, lags_ref, sems):
    share, lags = o_ref.shape[2:]
    period = lags // shards
    pieces = period // LANES
    members, hours, depth, _ = d_ref.shape
    total = members * depth // pieces
    lines = total // shards
    for m in range(members):
        rows[m * depth : (m + 1) * depth] = sum(d_ref[m, h].astype(jnp.float32) for h in range(hours))
    daily = []
    for k in range(pieces):
        column = [rows[pl.ds(r * pieces + k, shards, stride=lines * pieces), :] for r in range(lines)]
        daily.append(jnp.concatenate(column, axis=0).astype(jnp.bfloat16))
    half = pieces // 2
    daily = jnp.concatenate([jnp.concatenate(daily[c * half : (c + 1) * half], axis=1) for c in range(2)], axis=0)
    run = period // 2
    middle = jnp.dot(daily, first_ref[:run], preferred_element_type=jnp.float32)
    re = (middle[:total, :period] - middle[total:, period:]).reshape(lines, shards, period)
    im = (middle[:total, period:] + middle[total:, :period]).reshape(lines, shards, period)
    turn = first_ref[run : run + 2 * shards].astype(jnp.float32)
    turn = turn[:shards] + turn[shards:]
    cos, sin = turn[None, :, :period], turn[None, :, period:]
    turned = jnp.concatenate(
        [
            (re * cos - im * sin).reshape(total, period).astype(jnp.bfloat16),
            (re * sin + im * cos).reshape(total, period).astype(jnp.bfloat16),
        ],
        axis=0,
    )
    cuts = sems.shape[0]
    depth = total // cuts
    copies = []
    for cut in range(cuts):
        joined = jnp.dot(second_ref[cut * depth : (cut + 1) * depth], turned, preferred_element_type=jnp.float32)
        base = cut * (lags // cuts)
        for a in range(shards // cuts):
            for n in range(PARTS * PARTS):
                first = (a * PARTS * PARTS + n) * share
                value = joined[first : first + share].astype(jnp.bfloat16)
                lags_ref[n // PARTS, n % PARTS, :, base + a * period : base + (a + 1) * period] = value
        window = (slice(None),) * 3 + (pl.ds(base, lags // cuts),)
        copies.append(pltpu.make_async_copy(lags_ref.at[window], o_ref.at[window], sems.at[cut]))
        copies[-1].start()
    for copy in copies:
        copy.wait()


def lag_tables(bins, shards, share):
    lags = 2 * bins
    period = lags // shards
    lines = share * PARTS * PARTS
    lane = np.arange(LANES)
    inner = lane % shards * (LANES // shards) + lane // shards
    k = (np.arange(0, bins // shards, LANES)[:, None] + inner).reshape(-1, 1)
    b = np.arange(period)[None, :]
    d = np.arange(shards)[:, None]

    def turns(angle):
        return np.concatenate([np.cos(angle), np.sin(angle)], axis=1)

    fine = turns(d * b * (2.0 * math.pi / lags)) * bins**-0.5
    high = fine.astype(jnp.bfloat16).astype(np.float64)
    first = np.concatenate([turns((k * b % period) * (2.0 * math.pi / period)), high, fine - high])
    a = np.arange(shards)[:, None] - bins // period
    turn = (a * d.T % shards) * (2.0 * math.pi / shards)
    same = np.eye(lines).reshape(share, PARTS * PARTS, lines).transpose(1, 0, 2)
    second = [np.einsum("ad,nur->anurd", table, same) for table in (np.cos(turn), -np.sin(turn))]
    second = np.concatenate([table.reshape(lines * shards, -1) for table in second], axis=1)
    return jnp.asarray(first, jnp.bfloat16), jnp.asarray(second, jnp.bfloat16)


def body(spectra, pair_blocks, block_count):
    _, _, segments, parts, _, bins = spectra.shape
    slots = pair_blocks.shape[1]
    hours, stations = lax.axis_size("tm"), lax.axis_size("sta")
    near = 2 * CORES if stations % (2 * CORES) == 0 else CORES
    early = 2 if hours % 2 == 0 else 1
    late = hours // early
    shards = late * near
    share = slots // hours
    run = bins // shards
    halves = run // LANES
    chunk_in = segments * halves * 2 * parts
    chunk_out = share * parts * parts * 2 * halves
    order = first_order(late, stations)
    shard_of = second_order(late, near)
    classes = [shard_of.index((t, s % near)) for t, s in order]
    first, second = lag_tables(bins, shards, share)
    band = kernel_call(band_kernel, pltpu.VMEM((3 * LANES, LANES), jnp.bfloat16), [], [], weight=4)()
    band, block_count = lax.optimization_barrier((band, block_count))
    white = kernel_call(
        functools.partial(whiten_kernel, classes, shards, segments),
        pltpu.VMEM((late * stations, chunk_in + SLAB, LANES), jnp.bfloat16),
        [VMEM, pl.BlockSpec(memory_space=pltpu.HBM), pl.BlockSpec(memory_space=pltpu.SMEM), VMEM],
        [
            pltpu.VMEM((shards, chunk_in, LANES), jnp.float32),
            pltpu.VMEM((2, slots), jnp.int32),
            pltpu.SemaphoreType.DMA,
        ],
    )(
        placed(spectra.reshape(segments * parts, 2, bins), pltpu.VMEM),
        placed(pair_blocks[0].T, pltpu.HBM),
        block_count,
        band,
    )
    groups = [[(h * late + t) * stations + s for t, s in order] for h in range(early)]
    every = lax.all_to_all(white, MESH_AXES, 0, 0, tiled=True, axis_index_groups=groups)

    daily = kernel_call(
        functools.partial(cross_kernel, segments, share, near),
        pltpu.VMEM((hours * near, chunk_out, LANES), jnp.bfloat16),
        [VMEM],
        [pltpu.VMEM((hours * near * chunk_out, LANES), jnp.float32)],
    )(every.reshape(late, stations, chunk_in + SLAB, LANES))

    order = second_order(hours, near)
    groups = [[t * stations + s + m for t, m in order] for s in range(0, stations, near)]
    whole = lax.all_to_all(daily, MESH_AXES, 0, 0, tiled=True, axis_index_groups=groups)

    result = kernel_call(
        functools.partial(lag_kernel, shards),
        jax.ShapeDtypeStruct((parts, parts, share, 2 * bins), jnp.bfloat16),
        [VMEM] * 3,
        [
            pltpu.VMEM((shards * chunk_out, LANES), jnp.float32),
            pltpu.VMEM((parts, parts, share, 2 * bins), jnp.bfloat16),
            pltpu.SemaphoreType.DMA((2,)),
        ],
        pl.BlockSpec(memory_space=pl.ANY),
    )(whole.reshape(near, early, late * chunk_out, LANES), first, second)
    return result.transpose(2, 0, 1, 3).reshape(1, share, 1, 1, parts, parts, 2 * bins)


def solution(mesh):
    specs = (P("tm", "sta", None, None, None, None), P("sta", None, None), P("sta"))
    return jax.shard_map(
        body,
        mesh=mesh,
        in_specs=specs,
        out_specs=P("sta", "tm", None, None, None, None, None),
        check_vma=False,
    )
```

```python
import functools
import math

import jax
import jax.numpy as jnp
import numpy as np
from jax import lax
from jax.experimental import pallas as pl
from jax.experimental.pallas import tpu as pltpu
from jax.sharding import PartitionSpec as P

SMOOTH = 64
LANES = 128
PARTS = 3
SLAB = 8

CORES = 2

epsilon = 1e-05
MESH_AXES = ("tm", "sta")
VMEM = pl.BlockSpec(memory_space=pltpu.VMEM)


placed = pltpu.with_memory_space_constraint


def kernel_call(kernel, out_shape, in_specs, scratch, out_spec=VMEM, weight=1):
    return pl.pallas_call(
        kernel,
        out_shape=out_shape,
        in_specs=in_specs,
        out_specs=jax.tree.map(lambda _: out_spec, out_shape),
        scratch_shapes=scratch,
        cost_estimate=pl.CostEstimate(flops=weight * 10**9, bytes_accessed=weight * 4 * 10**6, transcendentals=0),
        compiler_params=pltpu.CompilerParams(vmem_limit_bytes=40 * 1024 * 1024),
    )


def band_kernel(o_ref):
    apart = lax.broadcasted_iota(jnp.int32, (3 * LANES, LANES), 0) - LANES
    apart = apart - lax.broadcasted_iota(jnp.int32, (3 * LANES, LANES), 1)
    o_ref[...] = (jnp.abs(apart) <= SMOOTH).astype(jnp.bfloat16)


def whiten_kernel(
    classes, shards, segments, x_ref, pairs_ref, count_ref, band_ref, o_ref, rows, pairs, sem
):
    pairs_copy = pltpu.make_async_copy(pairs_ref, pairs, sem)
    pairs_copy.start()
    bins = x_ref.shape[2]
    tiles = bins // LANES
    lane = lax.broadcasted_iota(jnp.int32, (SLAB, LANES), 1)
    even = lax.broadcasted_iota(jnp.int32, (SLAB, LANES), 0) % 2 == 0
    turn = [lane % shards == k for k in range(shards)]
    blank = jnp.zeros((SLAB, LANES), jnp.float32)
    band = band_ref[...]
    values, blocks = [], []
    for g in range(segments):
        lines = [x_ref[g * PARTS + x].astype(jnp.float32) for x in range(PARTS)]
        lines = jnp.concatenate(lines + [jnp.zeros((SLAB - 2 * PARTS, bins), jnp.float32)], axis=0)
        value = [lines[:, v * LANES : (v + 1) * LANES] for v in range(tiles)]
        size = [blank]
        for v in range(tiles):
            square = value[v] * value[v]
            twin = jnp.where(even, pltpu.roll(square, SLAB - 1, 0), pltpu.roll(square, 1, 0))
            size.append(jnp.sqrt(square + twin))
        size.append(blank)
        values.append(value)
        blocks += [jnp.concatenate(size[v : v + 3], axis=1) for v in range(tiles)]
    stacked = jnp.concatenate(blocks, axis=0)
    high = stacked.astype(jnp.bfloat16)
    low = (stacked - high.astype(jnp.float32)).astype(jnp.bfloat16)
    window = jnp.dot(high, band, preferred_element_type=jnp.float32) + jnp.dot(
        low, band, preferred_element_type=jnp.float32
    )
    halves = tiles // shards
    for g in range(segments):
        for j in range(halves):
            moved = []
            for i in range(shards):
                v = j * shards + i
                place = lane + v * LANES
                count = jnp.minimum(place + SMOOTH, bins - 1) - jnp.maximum(place - SMOOTH, 0) + 1
                first = (g * tiles + v) * SLAB
                smoothed = window[first : first + SLAB] / count.astype(jnp.float32)
                white = values[g][v] / (smoothed + epsilon)
                moved.append(pltpu.roll(white, i, 1) if i else white)
            first = (g * halves + j) * 2 * PARTS
            for d in range(shards):
                mixed = moved[0]
                for i in range(1, shards):
                    mixed = jnp.where(turn[(d + i) % shards], moved[i], mixed)
                if d:
                    mixed = pltpu.roll(mixed, LANES - d, 1)
                rows[d, first : first + 2 * PARTS] = mixed[: 2 * PARTS]
    packed = rows[...].astype(jnp.bfloat16)
    pairs_copy.wait()
    slots = pairs.shape[1]
    lists = jnp.concatenate([pairs[...].astype(jnp.float32), jnp.zeros((2, LANES - slots), jnp.float32)], axis=1)
    counts = jnp.full((SLAB - 2, LANES), count_ref[0].astype(jnp.float32))
    lists = jnp.concatenate([lists, counts], axis=0).astype(jnp.bfloat16)
    lines = rows.shape[1]
    for place, d in enumerate(classes):
        o_ref[place, :lines] = packed[d]
        o_ref[place, lines:] = lists


def station_columns(lists, hours, share):
    near = len(lists)
    group = hours * near
    rows = share * group
    lane = lax.broadcasted_iota(jnp.int32, (rows, LANES), 1)
    row = lax.broadcasted_iota(jnp.int32, (rows, LANES), 0)
    place = group - 1 - row % group
    owner = place // hours % (near // CORES) * CORES + place // (hours * (near // CORES))
    slot = place % hours * share + row // group
    columns = []
    for side in range(3):
        value = jnp.broadcast_to(lists[0][side : side + 1], lane.shape)
        for n in range(1, near):
            value = jnp.where(owner == n, lists[n][side : side + 1], value)
        columns.append(jnp.sum(jnp.where(lane == slot, value, 0.0), axis=1, keepdims=True).astype(jnp.int32))
    live = slot[:, :1] < columns[2]
    return [jnp.where(live, column, -1) for column in columns[:2]]


def first_order(hours, stations):
    chips = stations // CORES
    middle = chips // 2
    along = [*range(middle, -1, -1), *range(middle + 1, chips)]
    return [(t, z * CORES + core) for t in reversed(range(hours)) for z in along for core in reversed(range(CORES))]


def second_order(hours, near):
    order = [(t, z * CORES + core) for core in range(CORES) for z in range(near // CORES) for t in range(hours)]
    return order[::-1]


def cross_kernel(segments, share, near, w_ref, o_ref, rows):
    hours, stations, lines, _ = w_ref.shape
    blocks = lines - SLAB
    depth = stations * blocks
    group, chunk, _ = o_ref.shape
    slots = group * share
    halves = chunk // (share * PARTS * PARTS * 2)
    place_of = [station for _, station in first_order(1, stations)]
    place_of = [place_of.index(station) for station in range(stations)]
    cluster = lax.axis_index("sta") // near
    lists = []
    for n in range(near):
        place = 0
        for m in range(stations // near):
            place = jnp.where(cluster == m, place_of[m * near + n], place)
        lists.append(w_ref[0, pl.ds(place, 1), blocks:].reshape(SLAB, LANES).astype(jnp.float32))
    column = lax.broadcasted_iota(jnp.int32, (slots, depth), 1)
    sides = []
    for station in station_columns(lists, group // near, share):
        first = jnp.full(station.shape, depth)
        for m in range(stations):
            first = jnp.where(station == m, place_of[m] * blocks, first)
        offset = column - first
        sides.append([(offset == r).astype(jnp.bfloat16) for r in range(blocks)])
    chosen = jnp.concatenate(sides[0] + sides[1], axis=0)
    columns = [w_ref[h, :, :blocks].reshape(depth, LANES) for h in range(hours)]
    picked = []
    for m in range(0, len(columns), 2):
        two = jnp.concatenate(columns[m : m + 2], axis=1)
        two = jnp.dot(chosen, two, preferred_element_type=jnp.float32)
        picked += [two[:, n : n + LANES] for n in range(0, two.shape[1], LANES)]

    def part(side, h, g, j, c, x):
        first = (side * blocks + ((g * halves + j) * PARTS + x) * 2 + c) * slots
        return picked[h][first : first + slots]

    for j in range(halves):
        real = [None] * (PARTS * PARTS)
        imag = [None] * (PARTS * PARTS)
        for h in range(hours):
            for g in range(segments):
                left = [[part(0, h, g, j, c, x) for x in range(PARTS)] for c in range(2)]
                right = [[part(1, h, g, j, c, x) for x in range(PARTS)] for c in range(2)]
                for x in range(PARTS):
                    for y in range(PARTS):
                        re = left[0][x] * right[0][y] + left[1][x] * right[1][y]
                        im = left[0][x] * right[1][y] - left[1][x] * right[0][y]
                        n = x * PARTS + y
                        real[n] = re if real[n] is None else real[n] + re
                        imag[n] = im if imag[n] is None else imag[n] + im
        for n in range(PARTS * PARTS):
            for c, total in enumerate((real[n], imag[n])):
                for u in range(share):
                    row = ((n * share + u) * 2 + c) * halves + j
                    rows[pl.ds(row, group, stride=chunk), :] = total[u * group : (u + 1) * group]
    o_ref[...] = rows[...].reshape(o_ref.shape).astype(jnp.bfloat16)


def real_sums(re, im):
    n = len(re)
    if n == 1:
        return re
    half = n // 2
    even, odd = [], []
    for d in range(half):
        even.append((re[d] + re[d + half], im[d] + im[d + half]))
        x, y = re[d] - re[d + half], im[d] - im[d + half]
        if d == 0:
            odd.append((x, y))
        elif 4 * d == n:
            odd.append((-y, x))
        else:
            cos, sin = math.cos(2.0 * math.pi * d / n), math.sin(2.0 * math.pi * d / n)
            odd.append((x * cos - y * sin, x * sin + y * cos))
    sums = [real_sums(*map(list, zip(*values))) for values in (even, odd)]
    return [sums[a % 2][a // 2] for a in range(n)]


def lag_kernel(shards, share, d_ref, table_ref, o_ref, rows, lags_ref, sem):
    period = o_ref.shape[3] // shards
    pieces = period // LANES
    members, hours, depth, _ = d_ref.shape
    lines = share * PARTS * PARTS
    padded = -(-lines // SLAB) * SLAB
    for m in range(members):
        rows[m * depth : (m + 1) * depth] = sum(d_ref[m, h].astype(jnp.float32) for h in range(hours))
    if padded > lines:
        rows[members * depth :] = jnp.zeros((rows.shape[0] - members * depth, LANES), jnp.float32)
    half = pieces // 2
    daily = []
    for c in range(2):
        for d in range(shards):
            first = d * lines * pieces + c * half
            line = [rows[pl.ds(first + j, padded, stride=pieces), :] for j in range(half)]
            daily.append(jnp.concatenate(line, axis=1))
    daily = jnp.concatenate(daily, axis=0).astype(jnp.bfloat16)
    run = period // 2
    middle = jnp.dot(daily, table_ref[:run], preferred_element_type=jnp.float32)
    turn = table_ref[run : run + 2 * shards].astype(jnp.float32)
    turn = turn[:shards] + turn[shards:]
    total = shards * padded
    re, im = [], []
    for d in range(shards):
        first = d * padded
        with_re, with_im = middle[first : first + padded], middle[total + first : total + first + padded]
        x = with_re[:, :period] - with_im[:, period:]
        y = with_re[:, period:] + with_im[:, :period]
        cos, sin = turn[d : d + 1, :period], turn[d : d + 1, period:]
        re.append(x * cos - y * sin)
        im.append(x * sin + y * cos)
    sums = real_sums(re, im)
    for a in range(shards):
        value = sums[(a + shards // 2) % shards]
        for n in range(PARTS * PARTS):
            lags_ref[n // PARTS, n % PARTS, :, a * period : (a + 1) * period] = value[n * share : (n + 1) * share].astype(
                jnp.bfloat16
            )
    copy = pltpu.make_async_copy(lags_ref, o_ref, sem)
    copy.start()
    copy.wait()


def lag_table(bins, shards):
    lags = 2 * bins
    period = lags // shards
    lane = np.arange(LANES)
    inner = lane % shards * (LANES // shards) + lane // shards
    k = (np.arange(0, bins // shards, LANES)[:, None] + inner).reshape(-1, 1)
    b = np.arange(period)[None, :]
    d = np.arange(shards)[:, None]

    def turns(angle):
        return np.concatenate([np.cos(angle), np.sin(angle)], axis=1)

    fine = turns(d * b * (2.0 * math.pi / lags)) * bins**-0.5
    high = fine.astype(jnp.bfloat16).astype(np.float64)
    table = np.concatenate([turns((k * b % period) * (2.0 * math.pi / period)), high, fine - high])
    return jnp.asarray(table, jnp.bfloat16)


def body(spectra, pair_blocks, block_count):
    _, _, segments, parts, _, bins = spectra.shape
    slots = pair_blocks.shape[1]
    hours, stations = lax.axis_size("tm"), lax.axis_size("sta")
    near = 2 * CORES if stations % (2 * CORES) == 0 else CORES
    early = 2 if hours % 2 == 0 else 1
    late = hours // early
    shards = late * near
    share = slots // hours
    run = bins // shards
    halves = run // LANES
    chunk_in = segments * halves * 2 * parts
    chunk_out = share * parts * parts * 2 * halves
    order = first_order(late, stations)
    shard_of = second_order(late, near)
    classes = [shard_of.index((t, s % near)) for t, s in order]
    band = kernel_call(band_kernel, pltpu.VMEM((3 * LANES, LANES), jnp.bfloat16), [], [], weight=4)()
    band, block_count = lax.optimization_barrier((band, block_count))
    white = kernel_call(
        functools.partial(whiten_kernel, classes, shards, segments),
        pltpu.VMEM((late * stations, chunk_in + SLAB, LANES), jnp.bfloat16),
        [VMEM, pl.BlockSpec(memory_space=pltpu.HBM), pl.BlockSpec(memory_space=pltpu.SMEM), VMEM],
        [
            pltpu.VMEM((shards, chunk_in, LANES), jnp.float32),
            pltpu.VMEM((2, slots), jnp.int32),
            pltpu.SemaphoreType.DMA,
        ],
    )(
        placed(spectra.reshape(segments * parts, 2, bins), pltpu.VMEM),
        placed(pair_blocks[0].T, pltpu.HBM),
        block_count,
        band,
    )
    groups = [[(h * late + t) * stations + s for t, s in order] for h in range(early)]
    every = lax.all_to_all(white, MESH_AXES, 0, 0, tiled=True, axis_index_groups=groups)

    daily = kernel_call(
        functools.partial(cross_kernel, segments, share, near),
        pltpu.VMEM((hours * near, chunk_out, LANES), jnp.bfloat16),
        [VMEM],
        [pltpu.VMEM((hours * near * chunk_out, LANES), jnp.float32)],
    )(every.reshape(late, stations, chunk_in + SLAB, LANES))

    order = second_order(hours, near)
    groups = [[t * stations + s + m for t, m in order] for s in range(0, stations, near)]
    whole = lax.all_to_all(daily, MESH_AXES, 0, 0, tiled=True, axis_index_groups=groups)

    overrun = -(share * parts * parts) % SLAB * 2 * halves
    result = kernel_call(
        functools.partial(lag_kernel, shards, share),
        jax.ShapeDtypeStruct((parts, parts, share, 2 * bins), jnp.bfloat16),
        [VMEM] * 2,
        [
            pltpu.VMEM((shards * chunk_out + overrun, LANES), jnp.float32),
            pltpu.VMEM((parts, parts, share, 2 * bins), jnp.bfloat16),
            pltpu.SemaphoreType.DMA,
        ],
        pl.BlockSpec(memory_space=pl.ANY),
    )(whole.reshape(near, early, late * chunk_out, LANES), lag_table(bins, shards))
    return result.transpose(2, 0, 1, 3).reshape(1, share, 1, 1, parts, parts, 2 * bins)


def solution(mesh):
    specs = (P("tm", "sta", None, None, None, None), P("sta", None, None), P("sta"))
    return jax.shard_map(
        body,
        mesh=mesh,
        in_specs=specs,
        out_specs=P("sta", "tm", None, None, None, None, None),
        check_vma=False,
    )
```

```python
import functools
import math

import jax
import jax.numpy as jnp
import numpy as np
from jax import lax
from jax.experimental import pallas as pl
from jax.experimental.pallas import tpu as pltpu
from jax.sharding import PartitionSpec as P

SMOOTH = 64
LANES = 128
PARTS = 3
SLAB = 8

CORES = 2

epsilon = 1e-05
MESH_AXES = ("tm", "sta")
VMEM = pl.BlockSpec(memory_space=pltpu.VMEM)


placed = pltpu.with_memory_space_constraint


def kernel_call(kernel, out_shape, in_specs, scratch, out_spec=VMEM, weight=1):
    return pl.pallas_call(
        kernel,
        out_shape=out_shape,
        in_specs=in_specs,
        out_specs=jax.tree.map(lambda _: out_spec, out_shape),
        scratch_shapes=scratch,
        cost_estimate=pl.CostEstimate(flops=weight * 10**9, bytes_accessed=weight * 4 * 10**6, transcendentals=0),
        compiler_params=pltpu.CompilerParams(vmem_limit_bytes=40 * 1024 * 1024),
    )


def band_kernel(o_ref):
    apart = lax.broadcasted_iota(jnp.int32, (3 * LANES, LANES), 0) - LANES
    apart = apart - lax.broadcasted_iota(jnp.int32, (3 * LANES, LANES), 1)
    o_ref[...] = (jnp.abs(apart) <= SMOOTH).astype(jnp.bfloat16)


def whiten_kernel(
    classes, shards, segments, x_ref, pairs_ref, count_ref, band_ref, o_ref, rows, pairs, sem
):
    pairs_copy = pltpu.make_async_copy(pairs_ref, pairs, sem)
    pairs_copy.start()
    bins = x_ref.shape[2]
    tiles = bins // LANES
    lane = lax.broadcasted_iota(jnp.int32, (SLAB, LANES), 1)
    even = lax.broadcasted_iota(jnp.int32, (SLAB, LANES), 0) % 2 == 0
    turn = [lane % shards == k for k in range(shards)]
    blank = jnp.zeros((SLAB, LANES), jnp.float32)
    band = band_ref[...]
    values, blocks = [], []
    for g in range(segments):
        lines = [x_ref[g * PARTS + x].astype(jnp.float32) for x in range(PARTS)]
        lines = jnp.concatenate(lines + [jnp.zeros((SLAB - 2 * PARTS, bins), jnp.float32)], axis=0)
        value = [lines[:, v * LANES : (v + 1) * LANES] for v in range(tiles)]
        size = [blank]
        for v in range(tiles):
            square = value[v] * value[v]
            twin = jnp.where(even, pltpu.roll(square, SLAB - 1, 0), pltpu.roll(square, 1, 0))
            size.append(jnp.sqrt(square + twin))
        size.append(blank)
        values.append(value)
        blocks += [jnp.concatenate(size[v : v + 3], axis=1) for v in range(tiles)]
    stacked = jnp.concatenate(blocks, axis=0)
    high = stacked.astype(jnp.bfloat16)
    low = (stacked - high.astype(jnp.float32)).astype(jnp.bfloat16)
    window = jnp.dot(high, band, preferred_element_type=jnp.float32) + jnp.dot(
        low, band, preferred_element_type=jnp.float32
    )
    halves = tiles // shards
    for g in range(segments):
        for j in range(halves):
            moved = []
            for i in range(shards):
                v = j * shards + i
                place = lane + v * LANES
                count = jnp.minimum(place + SMOOTH, bins - 1) - jnp.maximum(place - SMOOTH, 0) + 1
                first = (g * tiles + v) * SLAB
                smoothed = window[first : first + SLAB] / count.astype(jnp.float32)
                white = values[g][v] / (smoothed + epsilon)
                moved.append(pltpu.roll(white, i, 1) if i else white)
            first = (g * halves + j) * 2 * PARTS
            for d in range(shards):
                mixed = moved[0]
                for i in range(1, shards):
                    mixed = jnp.where(turn[(d + i) % shards], moved[i], mixed)
                if d:
                    mixed = pltpu.roll(mixed, LANES - d, 1)
                rows[d, first : first + 2 * PARTS] = mixed[: 2 * PARTS]
    packed = rows[...].astype(jnp.bfloat16)
    pairs_copy.wait()
    slots = pairs.shape[1]
    lists = jnp.concatenate([pairs[...].astype(jnp.float32), jnp.zeros((2, LANES - slots), jnp.float32)], axis=1)
    counts = jnp.full((SLAB - 2, LANES), count_ref[0].astype(jnp.float32))
    lists = jnp.concatenate([lists, counts], axis=0).astype(jnp.bfloat16)
    lines = rows.shape[1]
    for place, d in enumerate(classes):
        o_ref[place, :lines] = packed[d]
        o_ref[place, lines:] = lists


def station_columns(lists, hours, share):
    near = len(lists)
    group = hours * near
    rows = share * group
    lane = lax.broadcasted_iota(jnp.int32, (rows, LANES), 1)
    row = lax.broadcasted_iota(jnp.int32, (rows, LANES), 0)
    place = group - 1 - row % group
    owner = place // hours % (near // CORES) * CORES + place // (hours * (near // CORES))
    slot = place % hours * share + row // group
    columns = []
    for side in range(3):
        value = jnp.broadcast_to(lists[0][side : side + 1], lane.shape)
        for n in range(1, near):
            value = jnp.where(owner == n, lists[n][side : side + 1], value)
        columns.append(jnp.sum(jnp.where(lane == slot, value, 0.0), axis=1, keepdims=True).astype(jnp.int32))
    live = slot[:, :1] < columns[2]
    return [jnp.where(live, column, -1) for column in columns[:2]]


def first_order(hours, stations):
    chips = stations // CORES
    middle = chips // 2
    along = [*range(middle, -1, -1), *range(middle + 1, chips)]
    return [(t, z * CORES + core) for t in reversed(range(hours)) for z in along for core in reversed(range(CORES))]


def second_order(hours, near):
    order = [(t, z * CORES + core) for core in range(CORES) for z in range(near // CORES) for t in range(hours)]
    return order[::-1]


def cross_kernel(segments, share, near, w_ref, o_ref, rows):
    hours, stations, lines, _ = w_ref.shape
    blocks = lines - SLAB
    depth = stations * blocks
    group, chunk, _ = o_ref.shape
    slots = group * share
    halves = chunk // (share * PARTS * PARTS * 2)
    place_of = [station for _, station in first_order(1, stations)]
    place_of = [place_of.index(station) for station in range(stations)]
    cluster = lax.axis_index("sta") // near
    lists = []
    for n in range(near):
        place = 0
        for m in range(stations // near):
            place = jnp.where(cluster == m, place_of[m * near + n], place)
        lists.append(w_ref[0, pl.ds(place, 1), blocks:].reshape(SLAB, LANES).astype(jnp.float32))
    column = lax.broadcasted_iota(jnp.int32, (slots, depth), 1)
    sides = []
    for station in station_columns(lists, group // near, share):
        first = jnp.full(station.shape, depth)
        for m in range(stations):
            first = jnp.where(station == m, place_of[m] * blocks, first)
        offset = column - first
        sides.append([(offset == r).astype(jnp.bfloat16) for r in range(blocks)])
    chosen = jnp.concatenate(sides[0] + sides[1], axis=0)
    columns = [w_ref[h, :, :blocks].reshape(depth, LANES) for h in range(hours)]
    picked = []
    for m in range(0, len(columns), 2):
        two = jnp.concatenate(columns[m : m + 2], axis=1)
        two = jnp.dot(chosen, two, preferred_element_type=jnp.float32)
        picked += [two[:, n : n + LANES] for n in range(0, two.shape[1], LANES)]

    def part(side, h, g, j, c, x):
        first = (side * blocks + ((g * halves + j) * PARTS + x) * 2 + c) * slots
        return picked[h][first : first + slots]

    for j in range(halves):
        real = [None] * (PARTS * PARTS)
        imag = [None] * (PARTS * PARTS)
        for h in range(hours):
            for g in range(segments):
                left = [[part(0, h, g, j, c, x) for x in range(PARTS)] for c in range(2)]
                right = [[part(1, h, g, j, c, x) for x in range(PARTS)] for c in range(2)]
                for x in range(PARTS):
                    for y in range(PARTS):
                        re = left[0][x] * right[0][y] + left[1][x] * right[1][y]
                        im = left[0][x] * right[1][y] - left[1][x] * right[0][y]
                        n = x * PARTS + y
                        real[n] = re if real[n] is None else real[n] + re
                        imag[n] = im if imag[n] is None else imag[n] + im
        for n in range(PARTS * PARTS):
            for c, total in enumerate((real[n], imag[n])):
                for u in range(share):
                    row = ((n * share + u) * 2 + c) * halves + j
                    rows[pl.ds(row, group, stride=chunk), :] = total[u * group : (u + 1) * group]
    o_ref[...] = rows[: group * chunk].reshape(o_ref.shape).astype(jnp.bfloat16)


def real_sums(re, im):
    n = len(re)
    if n == 1:
        return re
    half = n // 2
    even, odd = [], []
    for d in range(half):
        even.append((re[d] + re[d + half], im[d] + im[d + half]))
        x, y = re[d] - re[d + half], im[d] - im[d + half]
        if d == 0:
            odd.append((x, y))
        elif 4 * d == n:
            odd.append((-y, x))
        else:
            cos, sin = math.cos(2.0 * math.pi * d / n), math.sin(2.0 * math.pi * d / n)
            odd.append((x * cos - y * sin, x * sin + y * cos))
    sums = [real_sums(*map(list, zip(*values))) for values in (even, odd)]
    return [sums[a % 2][a // 2] for a in range(n)]


def lag_kernel(shards, share, d_ref, table_ref, o_ref, rows, lags_ref, sem):
    period = o_ref.shape[3] // shards
    pieces = period // LANES
    members, hours, depth, _ = d_ref.shape
    lines = share * PARTS * PARTS
    padded = -(-lines // SLAB) * SLAB
    for m in range(members):
        rows[m * depth : (m + 1) * depth] = sum(d_ref[m, h].astype(jnp.float32) for h in range(hours))
    if rows.shape[0] > members * depth:
        rows[members * depth :] = jnp.zeros((rows.shape[0] - members * depth, LANES), jnp.float32)
    half = pieces // 2
    daily = []
    for c in range(2):
        for d in range(shards):
            first = d * lines * pieces + c * half
            line = [rows[pl.ds(first + j, padded, stride=pieces), :] for j in range(half)]
            daily.append(jnp.concatenate(line, axis=1))
    daily = jnp.concatenate(daily, axis=0).astype(jnp.bfloat16)
    run = period // 2
    middle = jnp.dot(daily, table_ref[:run], preferred_element_type=jnp.float32)
    turn = table_ref[run : run + 2 * shards].astype(jnp.float32)
    turn = turn[:shards] + turn[shards:]
    total = shards * padded
    re, im = [], []
    for d in range(shards):
        first = d * padded
        with_re, with_im = middle[first : first + padded], middle[total + first : total + first + padded]
        x = with_re[:, :period] - with_im[:, period:]
        y = with_re[:, period:] + with_im[:, :period]
        cos, sin = turn[d : d + 1, :period], turn[d : d + 1, period:]
        re.append(x * cos - y * sin)
        im.append(x * sin + y * cos)
    sums = real_sums(re, im)
    for a in range(shards):
        value = sums[(a + shards // 2) % shards]
        for n in range(PARTS * PARTS):
            lags_ref[n // PARTS, n % PARTS, :, a * period : (a + 1) * period] = value[n * share : (n + 1) * share].astype(
                jnp.bfloat16
            )
    copy = pltpu.make_async_copy(lags_ref, o_ref, sem)
    copy.start()
    copy.wait()


def lag_table(bins, shards):
    lags = 2 * bins
    period = lags // shards
    lane = np.arange(LANES)
    inner = lane % shards * (LANES // shards) + lane // shards
    k = (np.arange(0, bins // shards, LANES)[:, None] + inner).reshape(-1, 1)
    b = np.arange(period)[None, :]
    d = np.arange(shards)[:, None]

    def turns(angle):
        return np.concatenate([np.cos(angle), np.sin(angle)], axis=1)

    fine = turns(d * b * (2.0 * math.pi / lags)) * bins**-0.5
    high = fine.astype(jnp.bfloat16).astype(np.float64)
    table = np.concatenate([turns((k * b % period) * (2.0 * math.pi / period)), high, fine - high])
    return jnp.asarray(table, jnp.bfloat16)


def body(spectra, pair_blocks, block_count):
    _, _, segments, parts, _, bins = spectra.shape
    slots = pair_blocks.shape[1]
    hours, stations = lax.axis_size("tm"), lax.axis_size("sta")
    near = 2 * CORES if stations % (2 * CORES) == 0 else CORES
    early = 2 if hours % 2 == 0 else 1
    late = hours // early
    shards = late * near
    share = slots // hours
    run = bins // shards
    halves = run // LANES
    chunk_in = segments * halves * 2 * parts
    chunk_out = share * parts * parts * 2 * halves
    order = first_order(late, stations)
    shard_of = second_order(late, near)
    classes = [shard_of.index((t, s % near)) for t, s in order]
    band = kernel_call(band_kernel, pltpu.VMEM((3 * LANES, LANES), jnp.bfloat16), [], [], weight=4)()
    band, block_count = lax.optimization_barrier((band, block_count))
    white = kernel_call(
        functools.partial(whiten_kernel, classes, shards, segments),
        pltpu.VMEM((late * stations, chunk_in + SLAB, LANES), jnp.bfloat16),
        [VMEM, pl.BlockSpec(memory_space=pltpu.HBM), pl.BlockSpec(memory_space=pltpu.SMEM), VMEM],
        [
            pltpu.VMEM((shards, chunk_in, LANES), jnp.float32),
            pltpu.VMEM((2, slots), jnp.int32),
            pltpu.SemaphoreType.DMA,
        ],
    )(
        placed(spectra.reshape(segments * parts, 2, bins), pltpu.VMEM),
        placed(pair_blocks[0].T, pltpu.HBM),
        block_count,
        band,
    )
    groups = [[(h * late + t) * stations + s for t, s in order] for h in range(early)]
    every = lax.all_to_all(white, MESH_AXES, 0, 0, tiled=True, axis_index_groups=groups)

    daily = kernel_call(
        functools.partial(cross_kernel, segments, share, near),
        pltpu.VMEM((hours * near, chunk_out, LANES), jnp.bfloat16),
        [VMEM],
        [pltpu.VMEM(((hours * near + 1) * chunk_out, LANES), jnp.float32)],
    )(every.reshape(late, stations, chunk_in + SLAB, LANES))

    order = second_order(hours, near)
    groups = [[t * stations + s + m for t, m in order] for s in range(0, stations, near)]
    whole = lax.all_to_all(daily, MESH_AXES, 0, 0, tiled=True, axis_index_groups=groups)

    overrun = (-(share * parts * parts) % SLAB + 2) * 2 * halves
    result = kernel_call(
        functools.partial(lag_kernel, shards, share),
        jax.ShapeDtypeStruct((parts, parts, share, 2 * bins), jnp.bfloat16),
        [VMEM] * 2,
        [
            pltpu.VMEM((shards * chunk_out + overrun, LANES), jnp.float32),
            pltpu.VMEM((parts, parts, share, 2 * bins), jnp.bfloat16),
            pltpu.SemaphoreType.DMA,
        ],
        pl.BlockSpec(memory_space=pl.ANY),
    )(whole.reshape(near, early, late * chunk_out, LANES), lag_table(bins, shards))
    return result.transpose(2, 0, 1, 3).reshape(1, share, 1, 1, parts, parts, 2 * bins)


def solution(mesh):
    specs = (P("tm", "sta", None, None, None, None), P("sta", None, None), P("sta"))
    return jax.shard_map(
        body,
        mesh=mesh,
        in_specs=specs,
        out_specs=P("sta", "tm", None, None, None, None, None),
        check_vma=False,
    )
```

```python
import functools
import math

import jax
import jax.numpy as jnp
import numpy as np
from jax import lax
from jax.experimental import pallas as pl
from jax.experimental.pallas import tpu as pltpu
from jax.sharding import PartitionSpec as P

SMOOTH = 64
LANES = 128
PARTS = 3
SLAB = 8

CORES = 2

epsilon = 1e-05
MESH_AXES = ("tm", "sta")
VMEM = pl.BlockSpec(memory_space=pltpu.VMEM)


placed = pltpu.with_memory_space_constraint


def kernel_call(kernel, out_shape, in_specs, scratch, out_spec=VMEM, weight=1):
    return pl.pallas_call(
        kernel,
        out_shape=out_shape,
        in_specs=in_specs,
        out_specs=jax.tree.map(lambda _: out_spec, out_shape),
        scratch_shapes=scratch,
        cost_estimate=pl.CostEstimate(flops=weight * 10**9, bytes_accessed=weight * 4 * 10**6, transcendentals=0),
        compiler_params=pltpu.CompilerParams(vmem_limit_bytes=40 * 1024 * 1024),
    )


def band_kernel(o_ref):
    apart = lax.broadcasted_iota(jnp.int32, (3 * LANES, LANES), 0) - LANES
    apart = apart - lax.broadcasted_iota(jnp.int32, (3 * LANES, LANES), 1)
    o_ref[...] = (jnp.abs(apart) <= SMOOTH).astype(jnp.bfloat16)


def whiten_kernel(
    classes, shards, segments, x_ref, pairs_ref, count_ref, band_ref, o_ref, rows, pairs, sem
):
    pairs_copy = pltpu.make_async_copy(pairs_ref, pairs, sem)
    pairs_copy.start()
    bins = x_ref.shape[2]
    tiles = bins // LANES
    lane = lax.broadcasted_iota(jnp.int32, (SLAB, LANES), 1)
    even = lax.broadcasted_iota(jnp.int32, (SLAB, LANES), 0) % 2 == 0
    turn = [lane % shards == k for k in range(shards)]
    blank = jnp.zeros((SLAB, LANES), jnp.float32)
    band = band_ref[...]
    values, blocks = [], []
    for g in range(segments):
        lines = [x_ref[g * PARTS + x].astype(jnp.float32) for x in range(PARTS)]
        lines = jnp.concatenate(lines + [jnp.zeros((SLAB - 2 * PARTS, bins), jnp.float32)], axis=0)
        value = [lines[:, v * LANES : (v + 1) * LANES] for v in range(tiles)]
        size = [blank]
        for v in range(tiles):
            square = value[v] * value[v]
            twin = jnp.where(even, pltpu.roll(square, SLAB - 1, 0), pltpu.roll(square, 1, 0))
            size.append(jnp.sqrt(square + twin))
        size.append(blank)
        values.append(value)
        blocks += [jnp.concatenate(size[v : v + 3], axis=1) for v in range(tiles)]
    stacked = jnp.concatenate(blocks, axis=0)
    high = stacked.astype(jnp.bfloat16)
    low = (stacked - high.astype(jnp.float32)).astype(jnp.bfloat16)
    window = jnp.dot(high, band, preferred_element_type=jnp.float32) + jnp.dot(
        low, band, preferred_element_type=jnp.float32
    )
    halves = tiles // shards
    for g in range(segments):
        for j in range(halves):
            moved = []
            for i in range(shards):
                v = j * shards + i
                place = lane + v * LANES
                count = jnp.minimum(place + SMOOTH, bins - 1) - jnp.maximum(place - SMOOTH, 0) + 1
                first = (g * tiles + v) * SLAB
                smoothed = window[first : first + SLAB] / count.astype(jnp.float32)
                white = values[g][v] / (smoothed + epsilon)
                moved.append(pltpu.roll(white, i, 1) if i else white)
            first = (g * halves + j) * 2 * PARTS
            for d in range(shards):
                mixed = moved[0]
                for i in range(1, shards):
                    mixed = jnp.where(turn[(d + i) % shards], moved[i], mixed)
                if d:
                    mixed = pltpu.roll(mixed, LANES - d, 1)
                rows[d, first : first + 2 * PARTS] = mixed[: 2 * PARTS]
    packed = rows[...].astype(jnp.bfloat16)
    pairs_copy.wait()
    slots = pairs.shape[1]
    lists = jnp.concatenate([pairs[...].astype(jnp.float32), jnp.zeros((2, LANES - slots), jnp.float32)], axis=1)
    counts = jnp.full((SLAB - 2, LANES), count_ref[0].astype(jnp.float32))
    lists = jnp.concatenate([lists, counts], axis=0).astype(jnp.bfloat16)
    lines = rows.shape[1]
    for place, d in enumerate(classes):
        o_ref[place, :lines] = packed[d]
        o_ref[place, lines:] = lists


def station_columns(lists, hours, share):
    near = len(lists)
    group = hours * near
    rows = share * group
    lane = lax.broadcasted_iota(jnp.int32, (rows, LANES), 1)
    row = lax.broadcasted_iota(jnp.int32, (rows, LANES), 0)
    place = group - 1 - row % group
    owner = place // hours % (near // CORES) * CORES + place // (hours * (near // CORES))
    slot = place % hours * share + row // group
    columns = []
    for side in range(3):
        value = jnp.broadcast_to(lists[0][side : side + 1], lane.shape)
        for n in range(1, near):
            value = jnp.where(owner == n, lists[n][side : side + 1], value)
        columns.append(jnp.sum(jnp.where(lane == slot, value, 0.0), axis=1, keepdims=True).astype(jnp.int32))
    live = slot[:, :1] < columns[2]
    return [jnp.where(live, column, -1) for column in columns[:2]]


def first_order(hours, stations):
    chips = stations // CORES
    middle = chips // 2
    along = [*range(middle, -1, -1), *range(middle + 1, chips)]
    return [(t, z * CORES + core) for t in reversed(range(hours)) for z in along for core in reversed(range(CORES))]


def second_order(hours, near):
    order = [(t, z * CORES + core) for core in range(CORES) for z in range(near // CORES) for t in range(hours)]
    return order[::-1]


def cross_kernel(segments, share, near, w_ref, o_ref, rows):
    hours, stations, lines, _ = w_ref.shape
    blocks = lines - SLAB
    depth = stations * blocks
    group, chunk, _ = o_ref.shape
    slots = group * share
    halves = chunk // (share * PARTS * PARTS * 2)
    place_of = [station for _, station in first_order(1, stations)]
    place_of = [place_of.index(station) for station in range(stations)]
    cluster = lax.axis_index("sta") // near
    lists = []
    for n in range(near):
        place = 0
        for m in range(stations // near):
            place = jnp.where(cluster == m, place_of[m * near + n], place)
        lists.append(w_ref[0, pl.ds(place, 1), blocks:].reshape(SLAB, LANES).astype(jnp.float32))
    column = lax.broadcasted_iota(jnp.int32, (slots, depth), 1)
    sides = []
    for station in station_columns(lists, group // near, share):
        first = jnp.full(station.shape, depth)
        for m in range(stations):
            first = jnp.where(station == m, place_of[m] * blocks, first)
        offset = column - first
        sides.append([(offset == r).astype(jnp.bfloat16) for r in range(blocks)])
    chosen = jnp.concatenate(sides[0] + sides[1], axis=0)
    columns = [w_ref[h, :, :blocks].reshape(depth, LANES) for h in range(hours)]
    picked = []
    for m in range(0, len(columns), 2):
        two = jnp.concatenate(columns[m : m + 2], axis=1)
        two = jnp.dot(chosen, two, preferred_element_type=jnp.float32)
        picked += [two[:, n : n + LANES] for n in range(0, two.shape[1], LANES)]

    def part(side, h, g, j, c, x):
        first = (side * blocks + ((g * halves + j) * PARTS + x) * 2 + c) * slots
        return picked[h][first : first + slots]

    for j in range(halves):
        real = [None] * (PARTS * PARTS)
        imag = [None] * (PARTS * PARTS)
        for h in range(hours):
            for g in range(segments):
                left = [[part(0, h, g, j, c, x) for x in range(PARTS)] for c in range(2)]
                right = [[part(1, h, g, j, c, x) for x in range(PARTS)] for c in range(2)]
                for x in range(PARTS):
                    for y in range(PARTS):
                        re = left[0][x] * right[0][y] + left[1][x] * right[1][y]
                        im = left[0][x] * right[1][y] - left[1][x] * right[0][y]
                        n = x * PARTS + y
                        real[n] = re if real[n] is None else real[n] + re
                        imag[n] = im if imag[n] is None else imag[n] + im
        for n in range(PARTS * PARTS):
            for c, total in enumerate((real[n], imag[n])):
                for u in range(share):
                    row = ((n * share + u) * 2 + c) * halves + j
                    rows[pl.ds(row, group, stride=chunk), :] = total[u * group : (u + 1) * group]
    o_ref[...] = rows[: group * chunk].reshape(o_ref.shape).astype(jnp.bfloat16)


def real_sums(re, im):
    n = len(re)
    if n == 1:
        return re
    half = n // 2
    even, odd = [], []
    for d in range(half):
        even.append((re[d] + re[d + half], im[d] + im[d + half]))
        x, y = re[d] - re[d + half], im[d] - im[d + half]
        if d == 0:
            odd.append((x, y))
        elif 4 * d == n:
            odd.append((-y, x))
        else:
            cos, sin = math.cos(2.0 * math.pi * d / n), math.sin(2.0 * math.pi * d / n)
            odd.append((x * cos - y * sin, x * sin + y * cos))
    sums = [real_sums(*map(list, zip(*values))) for values in (even, odd)]
    return [sums[a % 2][a // 2] for a in range(n)]


def lag_kernel(shards, share, d_ref, table_ref, o_ref, rows, lags_ref, sem):
    period = o_ref.shape[3] // shards
    pieces = period // LANES
    members, hours, depth, _ = d_ref.shape
    lines = share * PARTS * PARTS
    padded = -(-lines // SLAB) * SLAB
    for m in range(members):
        rows[m * depth : (m + 1) * depth] = sum(d_ref[m, h].astype(jnp.float32) for h in range(hours))
    if rows.shape[0] > members * depth:
        rows[members * depth :] = jnp.zeros((rows.shape[0] - members * depth, LANES), jnp.float32)
    daily = []
    for d in range(shards):
        first = d * lines * pieces
        line = [rows[pl.ds(first + k, padded, stride=pieces), :] for k in range(pieces)]
        daily.append(jnp.concatenate(line, axis=1))
    daily = jnp.concatenate(daily, axis=0).astype(jnp.bfloat16)
    middle = jnp.dot(daily, table_ref[:period], preferred_element_type=jnp.float32)
    turn = table_ref[period : period + 2 * shards].astype(jnp.float32)
    turn = turn[:shards] + turn[shards:]
    re, im = [], []
    for d in range(shards):
        x = middle[d * padded : (d + 1) * padded, :period]
        y = middle[d * padded : (d + 1) * padded, period:]
        cos, sin = turn[d : d + 1, :period], turn[d : d + 1, period:]
        re.append(x * cos - y * sin)
        im.append(x * sin + y * cos)
    sums = real_sums(re, im)
    for a in range(shards):
        value = sums[(a + shards // 2) % shards]
        for n in range(PARTS * PARTS):
            lags_ref[n // PARTS, n % PARTS, :, a * period : (a + 1) * period] = value[n * share : (n + 1) * share].astype(
                jnp.bfloat16
            )
    copy = pltpu.make_async_copy(lags_ref, o_ref, sem)
    copy.start()
    copy.wait()


def lag_table(bins, shards):
    lags = 2 * bins
    period = lags // shards
    lane = np.arange(LANES)
    inner = lane % shards * (LANES // shards) + lane // shards
    k = (np.arange(0, bins // shards, LANES)[:, None] + inner).reshape(-1, 1)
    b = np.arange(period)[None, :]
    d = np.arange(shards)[:, None]

    def turns(angle):
        return np.concatenate([np.cos(angle), np.sin(angle)], axis=1)

    fine = turns(d * b * (2.0 * math.pi / lags)) * bins**-0.5
    high = fine.astype(jnp.bfloat16).astype(np.float64)
    angle = (k * b % period) * (2.0 * math.pi / period)
    table = np.concatenate([turns(angle), turns(angle + math.pi / 2), high, fine - high])
    return jnp.asarray(table, jnp.bfloat16)


def body(spectra, pair_blocks, block_count):
    _, _, segments, parts, _, bins = spectra.shape
    slots = pair_blocks.shape[1]
    hours, stations = lax.axis_size("tm"), lax.axis_size("sta")
    near = 2 * CORES if stations % (2 * CORES) == 0 else CORES
    early = 2 if hours % 2 == 0 else 1
    late = hours // early
    shards = late * near
    share = slots // hours
    run = bins // shards
    halves = run // LANES
    chunk_in = segments * halves * 2 * parts
    chunk_out = share * parts * parts * 2 * halves
    order = first_order(late, stations)
    shard_of = second_order(late, near)
    classes = [shard_of.index((t, s % near)) for t, s in order]
    band = kernel_call(band_kernel, pltpu.VMEM((3 * LANES, LANES), jnp.bfloat16), [], [], weight=4)()
    band, block_count = lax.optimization_barrier((band, block_count))
    white = kernel_call(
        functools.partial(whiten_kernel, classes, shards, segments),
        pltpu.VMEM((late * stations, chunk_in + SLAB, LANES), jnp.bfloat16),
        [VMEM, pl.BlockSpec(memory_space=pltpu.HBM), pl.BlockSpec(memory_space=pltpu.SMEM), VMEM],
        [
            pltpu.VMEM((shards, chunk_in, LANES), jnp.float32),
            pltpu.VMEM((2, slots), jnp.int32),
            pltpu.SemaphoreType.DMA,
        ],
    )(
        placed(spectra.reshape(segments * parts, 2, bins), pltpu.VMEM),
        placed(pair_blocks[0].T, pltpu.HBM),
        block_count,
        band,
    )
    groups = [[(h * late + t) * stations + s for t, s in order] for h in range(early)]
    every = lax.all_to_all(white, MESH_AXES, 0, 0, tiled=True, axis_index_groups=groups)

    daily = kernel_call(
        functools.partial(cross_kernel, segments, share, near),
        pltpu.VMEM((hours * near, chunk_out, LANES), jnp.bfloat16),
        [VMEM],
        [pltpu.VMEM(((hours * near + 1) * chunk_out, LANES), jnp.float32)],
    )(every.reshape(late, stations, chunk_in + SLAB, LANES))

    order = second_order(hours, near)
    groups = [[t * stations + s + m for t, m in order] for s in range(0, stations, near)]
    whole = lax.all_to_all(daily, MESH_AXES, 0, 0, tiled=True, axis_index_groups=groups)

    overrun = (-(share * parts * parts) % SLAB + 2) * 2 * halves
    result = kernel_call(
        functools.partial(lag_kernel, shards, share),
        jax.ShapeDtypeStruct((parts, parts, share, 2 * bins), jnp.bfloat16),
        [VMEM] * 2,
        [
            pltpu.VMEM((shards * chunk_out + overrun, LANES), jnp.float32),
            pltpu.VMEM((parts, parts, share, 2 * bins), jnp.bfloat16),
            pltpu.SemaphoreType.DMA,
        ],
        pl.BlockSpec(memory_space=pl.ANY),
    )(whole.reshape(near, early, late * chunk_out, LANES), lag_table(bins, shards))
    return result.transpose(2, 0, 1, 3).reshape(1, share, 1, 1, parts, parts, 2 * bins)


def solution(mesh):
    specs = (P("tm", "sta", None, None, None, None), P("sta", None, None), P("sta"))
    return jax.shard_map(
        body,
        mesh=mesh,
        in_specs=specs,
        out_specs=P("sta", "tm", None, None, None, None, None),
        check_vma=False,
    )
```

```python
import functools
import math

import jax
import jax.numpy as jnp
import numpy as np
from jax import lax
from jax.experimental import pallas as pl
from jax.experimental.pallas import tpu as pltpu
from jax.sharding import PartitionSpec as P

SMOOTH = 64
LANES = 128
PARTS = 3
SLAB = 8

CORES = 2

epsilon = 1e-05
MESH_AXES = ("tm", "sta")
VMEM = pl.BlockSpec(memory_space=pltpu.VMEM)


placed = pltpu.with_memory_space_constraint


def kernel_call(kernel, out_shape, in_specs, scratch, out_spec=VMEM, weight=1):
    return pl.pallas_call(
        kernel,
        out_shape=out_shape,
        in_specs=in_specs,
        out_specs=jax.tree.map(lambda _: out_spec, out_shape),
        scratch_shapes=scratch,
        cost_estimate=pl.CostEstimate(flops=weight * 10**9, bytes_accessed=weight * 4 * 10**6, transcendentals=0),
        compiler_params=pltpu.CompilerParams(vmem_limit_bytes=40 * 1024 * 1024),
    )


def band_kernel(o_ref):
    apart = lax.broadcasted_iota(jnp.int32, (3 * LANES, LANES), 0) - LANES
    apart = apart - lax.broadcasted_iota(jnp.int32, (3 * LANES, LANES), 1)
    o_ref[...] = (jnp.abs(apart) <= SMOOTH).astype(jnp.bfloat16)


def whiten_kernel(
    classes, shards, segments, x_ref, pairs_ref, count_ref, band_ref, o_ref, rows, pairs, sem
):
    pairs_copy = pltpu.make_async_copy(pairs_ref, pairs, sem)
    pairs_copy.start()
    bins = x_ref.shape[2]
    tiles = bins // LANES
    lane = lax.broadcasted_iota(jnp.int32, (SLAB, LANES), 1)
    even = lax.broadcasted_iota(jnp.int32, (SLAB, LANES), 0) % 2 == 0
    turn = [lane % shards == k for k in range(shards)]
    blank = jnp.zeros((SLAB, LANES), jnp.float32)
    band = band_ref[...]
    values, blocks = [], []
    for g in range(segments):
        lines = [x_ref[g * PARTS + x].astype(jnp.float32) for x in range(PARTS)]
        lines = jnp.concatenate(lines + [jnp.zeros((SLAB - 2 * PARTS, bins), jnp.float32)], axis=0)
        value = [lines[:, v * LANES : (v + 1) * LANES] for v in range(tiles)]
        size = [blank]
        for v in range(tiles):
            square = value[v] * value[v]
            twin = jnp.where(even, pltpu.roll(square, SLAB - 1, 0), pltpu.roll(square, 1, 0))
            size.append(jnp.sqrt(square + twin))
        size.append(blank)
        values.append(value)
        blocks += [jnp.concatenate(size[v : v + 3], axis=1) for v in range(tiles)]
    stacked = jnp.concatenate(blocks, axis=0)
    high = stacked.astype(jnp.bfloat16)
    low = (stacked - high.astype(jnp.float32)).astype(jnp.bfloat16)
    window = jnp.dot(jnp.concatenate([high, low], axis=0), band, preferred_element_type=jnp.float32)
    window = window[: stacked.shape[0]] + window[stacked.shape[0] :]
    halves = tiles // shards
    for g in range(segments):
        for j in range(halves):
            moved = []
            for i in range(shards):
                v = j * shards + i
                place = lane + v * LANES
                count = jnp.minimum(place + SMOOTH, bins - 1) - jnp.maximum(place - SMOOTH, 0) + 1
                first = (g * tiles + v) * SLAB
                smoothed = window[first : first + SLAB] / count.astype(jnp.float32)
                white = values[g][v] / (smoothed + epsilon)
                moved.append(pltpu.roll(white, i, 1) if i else white)
            first = (g * halves + j) * 2 * PARTS
            for d in range(shards):
                mixed = moved[0]
                for i in range(1, shards):
                    mixed = jnp.where(turn[(d + i) % shards], moved[i], mixed)
                if d:
                    mixed = pltpu.roll(mixed, LANES - d, 1)
                rows[d, first : first + 2 * PARTS] = mixed[: 2 * PARTS]
    packed = rows[...].astype(jnp.bfloat16)
    lines = rows.shape[1]
    for place, d in enumerate(classes):
        o_ref[place, :lines] = packed[d]
    pairs_copy.wait()
    slots = pairs.shape[1]
    lists = jnp.concatenate([pairs[...].astype(jnp.float32), jnp.zeros((2, LANES - slots), jnp.float32)], axis=1)
    counts = jnp.full((SLAB - 2, LANES), count_ref[0].astype(jnp.float32))
    lists = jnp.concatenate([lists, counts], axis=0).astype(jnp.bfloat16)
    for place in range(len(classes)):
        o_ref[place, lines:] = lists


def station_columns(lists, hours, share):
    near = len(lists)
    group = hours * near
    rows = share * group
    lane = lax.broadcasted_iota(jnp.int32, (rows, LANES), 1)
    row = lax.broadcasted_iota(jnp.int32, (rows, LANES), 0)
    place = group - 1 - row % group
    owner = place // hours % (near // CORES) * CORES + place // (hours * (near // CORES))
    slot = place % hours * share + row // group
    columns = []
    for side in range(3):
        value = jnp.broadcast_to(lists[0][side : side + 1], lane.shape)
        for n in range(1, near):
            value = jnp.where(owner == n, lists[n][side : side + 1], value)
        columns.append(jnp.sum(jnp.where(lane == slot, value, 0.0), axis=1, keepdims=True).astype(jnp.int32))
    live = slot[:, :1] < columns[2]
    return [jnp.where(live, column, -1) for column in columns[:2]]


def first_order(hours, stations):
    chips = stations // CORES
    middle = chips // 2
    along = [*range(middle, -1, -1), *range(middle + 1, chips)]
    return [(t, z * CORES + core) for t in reversed(range(hours)) for z in along for core in reversed(range(CORES))]


def second_order(hours, near):
    order = [(t, z * CORES + core) for core in range(CORES) for z in range(near // CORES) for t in range(hours)]
    return order[::-1]


def cross_kernel(segments, share, near, w_ref, o_ref, rows):
    hours, stations, lines, _ = w_ref.shape
    blocks = lines - SLAB
    depth = stations * blocks
    group, chunk, _ = o_ref.shape
    slots = group * share
    halves = chunk // (share * PARTS * PARTS * 2)
    place_of = [station for _, station in first_order(1, stations)]
    place_of = [place_of.index(station) for station in range(stations)]
    cluster = lax.axis_index("sta") // near
    lists = []
    for n in range(near):
        place = 0
        for m in range(stations // near):
            place = jnp.where(cluster == m, place_of[m * near + n], place)
        lists.append(w_ref[0, pl.ds(place, 1), blocks:].reshape(SLAB, LANES).astype(jnp.float32))
    column = lax.broadcasted_iota(jnp.int32, (slots, depth), 1)
    sides = []
    for station in station_columns(lists, group // near, share):
        first = jnp.full(station.shape, depth)
        for m in range(stations):
            first = jnp.where(station == m, place_of[m] * blocks, first)
        offset = column - first
        sides.append([(offset == r).astype(jnp.bfloat16) for r in range(blocks)])
    chosen = jnp.concatenate(sides[0] + sides[1], axis=0)
    columns = [w_ref[h, :, :blocks].reshape(depth, LANES) for h in range(hours)]
    picked = []
    for m in range(0, len(columns), 2):
        two = jnp.concatenate(columns[m : m + 2], axis=1)
        two = jnp.dot(chosen, two, preferred_element_type=jnp.float32)
        picked += [two[:, n : n + LANES] for n in range(0, two.shape[1], LANES)]

    def part(side, h, g, j, c, x):
        first = (side * blocks + ((g * halves + j) * PARTS + x) * 2 + c) * slots
        return picked[h][first : first + slots]

    for j in range(halves):
        real = [None] * (PARTS * PARTS)
        imag = [None] * (PARTS * PARTS)
        for h in range(hours):
            for g in range(segments):
                left = [[part(0, h, g, j, c, x) for x in range(PARTS)] for c in range(2)]
                right = [[part(1, h, g, j, c, x) for x in range(PARTS)] for c in range(2)]
                for x in range(PARTS):
                    for y in range(PARTS):
                        re = left[0][x] * right[0][y] + left[1][x] * right[1][y]
                        im = left[0][x] * right[1][y] - left[1][x] * right[0][y]
                        n = x * PARTS + y
                        real[n] = re if real[n] is None else real[n] + re
                        imag[n] = im if imag[n] is None else imag[n] + im
        for n in range(PARTS * PARTS):
            for c, total in enumerate((real[n], imag[n])):
                for u in range(share):
                    row = ((n * share + u) * 2 + c) * halves + j
                    rows[pl.ds(row, group, stride=chunk), :] = total[u * group : (u + 1) * group]
    o_ref[...] = rows[: group * chunk].reshape(o_ref.shape).astype(jnp.bfloat16)


def real_sums(re, im):
    n = len(re)
    if n == 1:
        return re
    half = n // 2
    even, odd = [], []
    for d in range(half):
        even.append((re[d] + re[d + half], im[d] + im[d + half]))
        x, y = re[d] - re[d + half], im[d] - im[d + half]
        if d == 0:
            odd.append((x, y))
        elif 4 * d == n:
            odd.append((-y, x))
        else:
            cos, sin = math.cos(2.0 * math.pi * d / n), math.sin(2.0 * math.pi * d / n)
            odd.append((x * cos - y * sin, x * sin + y * cos))
    sums = [real_sums(*map(list, zip(*values))) for values in (even, odd)]
    return [sums[a % 2][a // 2] for a in range(n)]


def lag_kernel(shards, share, d_ref, table_ref, o_ref, rows, lags_ref, sem):
    period = o_ref.shape[3] // shards
    pieces = period // LANES
    members, hours, depth, _ = d_ref.shape
    lines = share * PARTS * PARTS
    padded = -(-lines // SLAB) * SLAB
    for m in range(members):
        rows[m * depth : (m + 1) * depth] = sum(d_ref[m, h].astype(jnp.float32) for h in range(hours))
    if rows.shape[0] > members * depth:
        rows[members * depth :] = jnp.zeros((rows.shape[0] - members * depth, LANES), jnp.float32)
    daily = []
    for d in range(shards):
        first = d * lines * pieces
        line = [rows[pl.ds(first + k, padded, stride=pieces), :] for k in range(pieces)]
        daily.append(jnp.concatenate(line, axis=1))
    daily = jnp.concatenate(daily, axis=0).astype(jnp.bfloat16)
    middle = jnp.dot(daily, table_ref[:period], preferred_element_type=jnp.float32)
    turn = table_ref[period : period + 2 * shards].astype(jnp.float32)
    turn = turn[:shards] + turn[shards:]
    re, im = [], []
    for d in range(shards):
        x = middle[d * padded : (d + 1) * padded, :period]
        y = middle[d * padded : (d + 1) * padded, period:]
        cos, sin = turn[d : d + 1, :period], turn[d : d + 1, period:]
        re.append(x * cos - y * sin)
        im.append(x * sin + y * cos)
    sums = real_sums(re, im)
    for a in range(shards):
        value = sums[(a + shards // 2) % shards]
        for n in range(PARTS * PARTS):
            lags_ref[n // PARTS, n % PARTS, :, a * period : (a + 1) * period] = value[n * share : (n + 1) * share].astype(
                jnp.bfloat16
            )
    copy = pltpu.make_async_copy(lags_ref, o_ref, sem)
    copy.start()
    copy.wait()


def lag_table(bins, shards):
    lags = 2 * bins
    period = lags // shards
    lane = np.arange(LANES)
    inner = lane % shards * (LANES // shards) + lane // shards
    k = (np.arange(0, bins // shards, LANES)[:, None] + inner).reshape(-1, 1)
    b = np.arange(period)[None, :]
    d = np.arange(shards)[:, None]

    def turns(angle):
        return np.concatenate([np.cos(angle), np.sin(angle)], axis=1)

    fine = turns(d * b * (2.0 * math.pi / lags)) * bins**-0.5
    high = fine.astype(jnp.bfloat16).astype(np.float64)
    angle = (k * b % period) * (2.0 * math.pi / period)
    table = np.concatenate([turns(angle), turns(angle + math.pi / 2), high, fine - high])
    return jnp.asarray(table, jnp.bfloat16)


def body(spectra, pair_blocks, block_count):
    _, _, segments, parts, _, bins = spectra.shape
    slots = pair_blocks.shape[1]
    hours, stations = lax.axis_size("tm"), lax.axis_size("sta")
    near = 2 * CORES if stations % (2 * CORES) == 0 else CORES
    early = 2 if hours % 2 == 0 else 1
    late = hours // early
    shards = late * near
    share = slots // hours
    run = bins // shards
    halves = run // LANES
    chunk_in = segments * halves * 2 * parts
    chunk_out = share * parts * parts * 2 * halves
    order = first_order(late, stations)
    shard_of = second_order(late, near)
    classes = [shard_of.index((t, s % near)) for t, s in order]
    band = kernel_call(band_kernel, pltpu.VMEM((3 * LANES, LANES), jnp.bfloat16), [], [], weight=4)()
    band, block_count = lax.optimization_barrier((band, block_count))
    white = kernel_call(
        functools.partial(whiten_kernel, classes, shards, segments),
        pltpu.VMEM((late * stations, chunk_in + SLAB, LANES), jnp.bfloat16),
        [VMEM, pl.BlockSpec(memory_space=pltpu.HBM), pl.BlockSpec(memory_space=pltpu.SMEM), VMEM],
        [
            pltpu.VMEM((shards, chunk_in, LANES), jnp.float32),
            pltpu.VMEM((2, slots), jnp.int32),
            pltpu.SemaphoreType.DMA,
        ],
    )(
        placed(spectra.reshape(segments * parts, 2, bins), pltpu.VMEM),
        placed(pair_blocks[0].T, pltpu.HBM),
        block_count,
        band,
    )
    groups = [[(h * late + t) * stations + s for t, s in order] for h in range(early)]
    every = lax.all_to_all(white, MESH_AXES, 0, 0, tiled=True, axis_index_groups=groups)

    daily = kernel_call(
        functools.partial(cross_kernel, segments, share, near),
        pltpu.VMEM((hours * near, chunk_out, LANES), jnp.bfloat16),
        [VMEM],
        [pltpu.VMEM(((hours * near + 1) * chunk_out, LANES), jnp.float32)],
    )(every.reshape(late, stations, chunk_in + SLAB, LANES))

    order = second_order(hours, near)
    groups = [[t * stations + s + m for t, m in order] for s in range(0, stations, near)]
    whole = lax.all_to_all(daily, MESH_AXES, 0, 0, tiled=True, axis_index_groups=groups)

    overrun = (-(share * parts * parts) % SLAB + 2) * 2 * halves
    result = kernel_call(
        functools.partial(lag_kernel, shards, share),
        jax.ShapeDtypeStruct((parts, parts, share, 2 * bins), jnp.bfloat16),
        [VMEM] * 2,
        [
            pltpu.VMEM((shards * chunk_out + overrun, LANES), jnp.float32),
            pltpu.VMEM((parts, parts, share, 2 * bins), jnp.bfloat16),
            pltpu.SemaphoreType.DMA,
        ],
        pl.BlockSpec(memory_space=pl.ANY),
    )(whole.reshape(near, early, late * chunk_out, LANES), lag_table(bins, shards))
    return result.transpose(2, 0, 1, 3).reshape(1, share, 1, 1, parts, parts, 2 * bins)


def solution(mesh):
    specs = (P("tm", "sta", None, None, None, None), P("sta", None, None), P("sta"))
    return jax.shard_map(
        body,
        mesh=mesh,
        in_specs=specs,
        out_specs=P("sta", "tm", None, None, None, None, None),
        check_vma=False,
    )
```

```python
import functools
import math

import jax
import jax.numpy as jnp
import numpy as np
from jax import lax
from jax.experimental import pallas as pl
from jax.experimental.pallas import tpu as pltpu
from jax.sharding import PartitionSpec as P

SMOOTH = 64
LANES = 128
PARTS = 3
SLAB = 8

CORES = 2

epsilon = 1e-05
MESH_AXES = ("tm", "sta")
VMEM = pl.BlockSpec(memory_space=pltpu.VMEM)


placed = pltpu.with_memory_space_constraint


def kernel_call(kernel, out_shape, in_specs, scratch, out_spec=VMEM, weight=1):
    return pl.pallas_call(
        kernel,
        out_shape=out_shape,
        in_specs=in_specs,
        out_specs=jax.tree.map(lambda _: out_spec, out_shape),
        scratch_shapes=scratch,
        cost_estimate=pl.CostEstimate(flops=weight * 10**9, bytes_accessed=weight * 4 * 10**6, transcendentals=0),
        compiler_params=pltpu.CompilerParams(vmem_limit_bytes=40 * 1024 * 1024),
    )


def band_kernel(o_ref):
    apart = lax.broadcasted_iota(jnp.int32, (3 * LANES, LANES), 0) - LANES
    apart = apart - lax.broadcasted_iota(jnp.int32, (3 * LANES, LANES), 1)
    o_ref[...] = (jnp.abs(apart) <= SMOOTH).astype(jnp.bfloat16)


def whiten_kernel(
    classes, shards, segments, x_ref, pairs_ref, count_ref, band_ref, o_ref, rows, pairs, sem
):
    pairs_copy = pltpu.make_async_copy(pairs_ref, pairs, sem)
    pairs_copy.start()
    bins = x_ref.shape[2]
    tiles = bins // LANES
    lane = lax.broadcasted_iota(jnp.int32, (SLAB, LANES), 1)
    even = lax.broadcasted_iota(jnp.int32, (SLAB, LANES), 0) % 2 == 0
    turn = [lane % shards == k for k in range(shards)]
    blank = jnp.zeros((SLAB, LANES), jnp.float32)
    band = band_ref[...]
    values, blocks = [], []
    for g in range(segments):
        lines = [x_ref[g * PARTS + x].astype(jnp.float32) for x in range(PARTS)]
        lines = jnp.concatenate(lines + [jnp.zeros((SLAB - 2 * PARTS, bins), jnp.float32)], axis=0)
        value = [lines[:, v * LANES : (v + 1) * LANES] for v in range(tiles)]
        size = [blank]
        for v in range(tiles):
            square = value[v] * value[v]
            twin = jnp.where(even, pltpu.roll(square, SLAB - 1, 0), pltpu.roll(square, 1, 0))
            size.append(jnp.sqrt(square + twin))
        size.append(blank)
        values.append(value)
        blocks += [jnp.concatenate(size[v : v + 3], axis=1) for v in range(tiles)]
    stacked = jnp.concatenate(blocks, axis=0)
    high = stacked.astype(jnp.bfloat16)
    low = (stacked - high.astype(jnp.float32)).astype(jnp.bfloat16)
    window = jnp.dot(jnp.concatenate([high, low], axis=0), band, preferred_element_type=jnp.float32)
    window = window[: stacked.shape[0]] + window[stacked.shape[0] :]
    halves = tiles // shards
    for g in range(segments):
        for j in range(halves):
            moved = []
            for i in range(shards):
                v = j * shards + i
                place = lane + v * LANES
                count = jnp.minimum(place + SMOOTH, bins - 1) - jnp.maximum(place - SMOOTH, 0) + 1
                first = (g * tiles + v) * SLAB
                smoothed = window[first : first + SLAB] / count.astype(jnp.float32)
                white = values[g][v] / (smoothed + epsilon)
                moved.append(pltpu.roll(white, i, 1) if i else white)
            first = (g * halves + j) * 2 * PARTS
            for d in range(shards):
                mixed = moved[0]
                for i in range(1, shards):
                    mixed = jnp.where(turn[(d + i) % shards], moved[i], mixed)
                if d:
                    mixed = pltpu.roll(mixed, LANES - d, 1)
                rows[d, first : first + 2 * PARTS] = mixed[: 2 * PARTS]
    packed = rows[...].astype(jnp.bfloat16)
    lines = rows.shape[1]
    for place, d in enumerate(classes):
        o_ref[place, :lines] = packed[d]
    pairs_copy.wait()
    slots = pairs.shape[1]
    lists = jnp.concatenate([pairs[...].astype(jnp.float32), jnp.zeros((2, LANES - slots), jnp.float32)], axis=1)
    counts = jnp.full((SLAB - 2, LANES), count_ref[0].astype(jnp.float32))
    lists = jnp.concatenate([lists, counts], axis=0).astype(jnp.bfloat16)
    for place in range(len(classes)):
        o_ref[place, lines:] = lists


def station_columns(lists, hours, share):
    near = len(lists)
    group = hours * near
    rows = share * group
    lane = lax.broadcasted_iota(jnp.int32, (rows, LANES), 1)
    row = lax.broadcasted_iota(jnp.int32, (rows, LANES), 0)
    place = group - 1 - row % group
    owner = place // hours % (near // CORES) * CORES + place // (hours * (near // CORES))
    slot = place % hours * share + row // group
    columns = []
    for side in range(3):
        value = jnp.broadcast_to(lists[0][side : side + 1], lane.shape)
        for n in range(1, near):
            value = jnp.where(owner == n, lists[n][side : side + 1], value)
        columns.append(jnp.sum(jnp.where(lane == slot, value, 0.0), axis=1, keepdims=True).astype(jnp.int32))
    live = slot[:, :1] < columns[2]
    return [jnp.where(live, column, -1) for column in columns[:2]]


def first_order(hours, stations):
    chips = stations // CORES
    middle = chips // 2
    along = [*range(middle, -1, -1), *range(middle + 1, chips)]
    return [(t, z * CORES + core) for t in reversed(range(hours)) for z in along for core in reversed(range(CORES))]


def second_order(hours, near):
    order = [(t, z * CORES + core) for core in range(CORES) for z in range(near // CORES) for t in range(hours)]
    return order[::-1]


def cross_kernel(segments, share, near, w_ref, o_ref, rows):
    hours, stations, lines, _ = w_ref.shape
    blocks = lines - SLAB
    depth = stations * blocks
    group, chunk, _ = o_ref.shape
    slots = group * share
    halves = chunk // (share * PARTS * PARTS * 2)
    place_of = [station for _, station in first_order(1, stations)]
    place_of = [place_of.index(station) for station in range(stations)]
    cluster = lax.axis_index("sta") // near
    lists = []
    for n in range(near):
        place = 0
        for m in range(stations // near):
            place = jnp.where(cluster == m, place_of[m * near + n], place)
        lists.append(w_ref[0, pl.ds(place, 1), blocks:].reshape(SLAB, LANES).astype(jnp.float32))
    column = lax.broadcasted_iota(jnp.int32, (slots, depth), 1)
    sides = []
    for station in station_columns(lists, group // near, share):
        first = jnp.full(station.shape, depth)
        for m in range(stations):
            first = jnp.where(station == m, place_of[m] * blocks, first)
        offset = column - first
        sides.append([(offset == r).astype(jnp.bfloat16) for r in range(blocks)])
    chosen = jnp.concatenate(sides[0] + sides[1], axis=0)
    columns = [w_ref[h, :, :blocks].reshape(depth, LANES) for h in range(hours)]
    picked = []
    for m in range(0, len(columns), 2):
        two = jnp.concatenate(columns[m : m + 2], axis=1)
        two = jnp.dot(chosen, two, preferred_element_type=jnp.float32)
        picked += [two[:, n : n + LANES] for n in range(0, two.shape[1], LANES)]

    def part(side, h, g, j, c, x):
        first = (side * blocks + ((g * halves + j) * PARTS + x) * 2 + c) * slots
        return picked[h][first : first + slots]

    for j in range(halves):
        real = [None] * (PARTS * PARTS)
        imag = [None] * (PARTS * PARTS)
        for h in range(hours):
            for g in range(segments):
                left = [[part(0, h, g, j, c, x) for x in range(PARTS)] for c in range(2)]
                right = [[part(1, h, g, j, c, x) for x in range(PARTS)] for c in range(2)]
                for x in range(PARTS):
                    for y in range(PARTS):
                        re = left[0][x] * right[0][y] + left[1][x] * right[1][y]
                        im = left[0][x] * right[1][y] - left[1][x] * right[0][y]
                        n = x * PARTS + y
                        real[n] = re if real[n] is None else real[n] + re
                        imag[n] = im if imag[n] is None else imag[n] + im
        for n in range(PARTS * PARTS):
            for c, total in enumerate((real[n], imag[n])):
                for u in range(share):
                    row = ((n * share + u) * 2 + c) * halves + j
                    rows[pl.ds(row, group, stride=chunk), :] = total[u * group : (u + 1) * group]
    o_ref[...] = rows[: group * chunk].reshape(o_ref.shape).astype(jnp.bfloat16)


def real_sums(re, im):
    n = len(re)
    if n == 1:
        return re
    half = n // 2
    even, odd = [], []
    for d in range(half):
        even.append((re[d] + re[d + half], im[d] + im[d + half]))
        x, y = re[d] - re[d + half], im[d] - im[d + half]
        if d == 0:
            odd.append((x, y))
        elif 4 * d == n:
            odd.append((-y, x))
        else:
            cos, sin = math.cos(2.0 * math.pi * d / n), math.sin(2.0 * math.pi * d / n)
            odd.append((x * cos - y * sin, x * sin + y * cos))
    sums = [real_sums(*map(list, zip(*values))) for values in (even, odd)]
    return [sums[a % 2][a // 2] for a in range(n)]


def lag_kernel(shards, share, d_ref, table_ref, o_ref, rows, lags_ref, sem):
    period = o_ref.shape[3] // shards
    pieces = period // LANES
    members, hours, depth, _ = d_ref.shape
    lines = share * PARTS * PARTS
    padded = -(-lines // SLAB) * SLAB
    for m in range(members):
        rows[m * depth : (m + 1) * depth] = sum(d_ref[m, h].astype(jnp.float32) for h in range(hours))
    if rows.shape[0] > members * depth:
        rows[members * depth :] = jnp.zeros((rows.shape[0] - members * depth, LANES), jnp.float32)
    daily = []
    for d in range(shards):
        first = d * lines * pieces
        line = [rows[pl.ds(first + k, padded, stride=pieces), :] for k in range(pieces)]
        daily.append(jnp.concatenate(line, axis=1))
    daily = jnp.concatenate(daily, axis=0).astype(jnp.bfloat16)
    middle = jnp.dot(daily, table_ref[:period], preferred_element_type=jnp.float32)
    turn = table_ref[period : period + 2 * shards].astype(jnp.float32)
    turn = turn[:shards] + turn[shards:]
    re, im = [], []
    for d in range(shards):
        x = middle[d * padded : (d + 1) * padded, :period]
        y = middle[d * padded : (d + 1) * padded, period:]
        cos, sin = turn[d : d + 1, :period], turn[d : d + 1, period:]
        re.append(x * cos - y * sin)
        im.append(x * sin + y * cos)
    sums = real_sums(re, im)
    for a in range(shards):
        value = sums[(a + shards // 2) % shards].astype(jnp.bfloat16)
        for n in range(PARTS * PARTS):
            lags_ref[n // PARTS, n % PARTS, :, a * period : (a + 1) * period] = value[n * share : (n + 1) * share]
    copy = pltpu.make_async_copy(lags_ref, o_ref, sem)
    copy.start()
    copy.wait()


def lag_table(bins, shards):
    lags = 2 * bins
    period = lags // shards
    lane = np.arange(LANES)
    inner = lane % shards * (LANES // shards) + lane // shards
    k = (np.arange(0, bins // shards, LANES)[:, None] + inner).reshape(-1, 1)
    b = np.arange(period)[None, :]
    d = np.arange(shards)[:, None]

    def turns(angle):
        return np.concatenate([np.cos(angle), np.sin(angle)], axis=1)

    fine = turns(d * b * (2.0 * math.pi / lags)) * bins**-0.5
    high = fine.astype(jnp.bfloat16).astype(np.float64)
    angle = (k * b % period) * (2.0 * math.pi / period)
    table = np.concatenate([turns(angle), turns(angle + math.pi / 2), high, fine - high])
    return jnp.asarray(table, jnp.bfloat16)


def body(spectra, pair_blocks, block_count):
    _, _, segments, parts, _, bins = spectra.shape
    slots = pair_blocks.shape[1]
    hours, stations = lax.axis_size("tm"), lax.axis_size("sta")
    near = 2 * CORES if stations % (2 * CORES) == 0 else CORES
    early = 2 if hours % 2 == 0 else 1
    late = hours // early
    shards = late * near
    share = slots // hours
    run = bins // shards
    halves = run // LANES
    chunk_in = segments * halves * 2 * parts
    chunk_out = share * parts * parts * 2 * halves
    order = first_order(late, stations)
    shard_of = second_order(late, near)
    classes = [shard_of.index((t, s % near)) for t, s in order]
    band = kernel_call(band_kernel, pltpu.VMEM((3 * LANES, LANES), jnp.bfloat16), [], [], weight=4)()
    band, block_count = lax.optimization_barrier((band, block_count))
    white = kernel_call(
        functools.partial(whiten_kernel, classes, shards, segments),
        pltpu.VMEM((late * stations, chunk_in + SLAB, LANES), jnp.bfloat16),
        [VMEM, pl.BlockSpec(memory_space=pltpu.HBM), pl.BlockSpec(memory_space=pltpu.SMEM), VMEM],
        [
            pltpu.VMEM((shards, chunk_in, LANES), jnp.float32),
            pltpu.VMEM((2, slots), jnp.int32),
            pltpu.SemaphoreType.DMA,
        ],
    )(
        placed(spectra.reshape(segments * parts, 2, bins), pltpu.VMEM),
        placed(pair_blocks[0].T, pltpu.HBM),
        block_count,
        band,
    )
    groups = [[(h * late + t) * stations + s for t, s in order] for h in range(early)]
    every = lax.all_to_all(white, MESH_AXES, 0, 0, tiled=True, axis_index_groups=groups)

    daily = kernel_call(
        functools.partial(cross_kernel, segments, share, near),
        pltpu.VMEM((hours * near, chunk_out, LANES), jnp.bfloat16),
        [VMEM],
        [pltpu.VMEM(((hours * near + 1) * chunk_out, LANES), jnp.float32)],
    )(every.reshape(late, stations, chunk_in + SLAB, LANES))

    order = second_order(hours, near)
    groups = [[t * stations + s + m for t, m in order] for s in range(0, stations, near)]
    whole = lax.all_to_all(daily, MESH_AXES, 0, 0, tiled=True, axis_index_groups=groups)

    overrun = (-(share * parts * parts) % SLAB + 2) * 2 * halves
    result = kernel_call(
        functools.partial(lag_kernel, shards, share),
        jax.ShapeDtypeStruct((parts, parts, share, 2 * bins), jnp.bfloat16),
        [VMEM] * 2,
        [
            pltpu.VMEM((shards * chunk_out + overrun, LANES), jnp.float32),
            pltpu.VMEM((parts, parts, share, 2 * bins), jnp.bfloat16),
            pltpu.SemaphoreType.DMA,
        ],
        pl.BlockSpec(memory_space=pl.ANY),
    )(whole.reshape(near, early, late * chunk_out, LANES), lag_table(bins, shards))
    return result.transpose(2, 0, 1, 3).reshape(1, share, 1, 1, parts, parts, 2 * bins)


def solution(mesh):
    specs = (P("tm", "sta", None, None, None, None), P("sta", None, None), P("sta"))
    return jax.shard_map(
        body,
        mesh=mesh,
        in_specs=specs,
        out_specs=P("sta", "tm", None, None, None, None, None),
        check_vma=False,
    )
```
